32 devices in a mesh: grp: 2 (over y), tm: 4 (over z), space: 2 (over x), obs: 2 (over core).
Axes of the slice: x: 2, y: 2, z: 4, core: 2. Of those that a mesh axis runs over, the one named last changes fastest.
Arguments:
- obs_panel: bfloat16 [8192, 768], P(('grp', 'tm', 'space', 'obs')), parts along dimension 0, may hold values from -0.375 to 0.375
- node_index: int32 [8192], P(('grp', 'tm', 'space', 'obs')), parts along dimension 0, may hold values from 0 to 767
- weight: bfloat16 [8192], P(('grp', 'tm', 'space', 'obs')), parts along dimension 0, may hold values from 0.049804688 to 0.5
- residual: bfloat16 [8192], P(('grp', 'tm', 'space', 'obs')), parts along dimension 0, may hold values from -6 to 6
- route_time: int32 [8192], P(('grp', 'tm', 'space', 'obs')), parts along dimension 0, may hold values from 0 to 3, as said below
- spatial_prec: float32 [8, 768, 768], P(('grp', 'tm'), ('space', 'obs')), parts along dimension 0, as said below
- ar_coef: float32 [8], P(('grp', 'tm')), parts along dimension 0, may hold values from 0.5 to 0.85
- prior_rhs: float32 [8, 768], P(('grp', 'tm'), ('space', 'obs')), parts along dimension 0, may hold values from -6 to 6
Outputs:
- reduced_diag: float32 [8, 768, 768], P(('grp', 'tm'), ('space', 'obs')), parts along dimension 0
- fill_block: float32 [8, 768, 768], P(('grp', 'tm'), ('space', 'obs')), parts along dimension 0
- reduced_rhs: float32 [8, 768], P(('grp', 'tm'), ('space', 'obs')), parts along dimension 0
The draws below stay inside these ranges and needn't reach their ends.
There are 2 independent parts, one for each index of `grp`. The reference program is written for one: setup_inputs(seed, part) draws one part's arguments, and reference() takes and returns one part's arrays. A program takes and returns all parts, laid end to end along the dimension named above; each array names one. Nothing has to cross between parts.
Inputs may be any that keep to these rules, and one draw needn't show every extreme that they name: `route_time`: each device's 256 rows name each time block at most 128 times; in every draw one time block receives exactly 128 rows from every device's block of rows. `spatial_prec`: each block is symmetric positive definite.
All inputs are finite; a program needn't handle non-finite values.
Results may differ from the reference program's by a relative error of at most 0.0044.
Values may be sent and summed in bfloat16 or wider, within the bound.
A program may use at most 64 MiB of HBM per device.

```python
import math
import jax
import jax.numpy as jnp
from jax import lax

B = 768
ROWS_DEV = 256
NT = 4
SOURCES = 16
ROWS_ALL = 4096
ROWS_TIME = 1024
CAP = 128


def draw_route_time(key, part):
    full_time = jax.random.randint(jax.random.fold_in(key, 201), (), 0, NT).astype(jnp.int32)
    others_count = ROWS_DEV - CAP

    def one_source(source_index):
        source_key = jax.random.fold_in(key, source_index + 300)
        slot_picks = jax.random.permutation(jax.random.fold_in(source_key, 1), (NT - 1) * CAP)[:others_count]
        other_time = (slot_picks // CAP).astype(jnp.int32)
        other_time = other_time + (other_time >= full_time).astype(jnp.int32)
        row_times = jnp.concatenate([jnp.full((CAP,), full_time, jnp.int32), other_time])
        shuffle = jax.random.permutation(jax.random.fold_in(source_key, 2), ROWS_DEV)
        return row_times[shuffle]
    return jax.vmap(one_source)(jnp.arange(SOURCES, dtype=jnp.int32)).reshape(ROWS_ALL)


def draw_spatial_prec(key, part):
    mixing_key = jax.random.fold_in(key, 101)
    base_key = jax.random.fold_in(key, 102)
    mixing = jax.random.normal(mixing_key, (NT, B, B), jnp.float32)
    base_diag = jax.random.uniform(base_key, (NT, B), jnp.float32, 1.0, 3.0)
    product = jnp.einsum('tik,tjk->tij', mixing, mixing, precision=lax.Precision.HIGHEST) / B
    symmetric = 0.5 * (product + jnp.swapaxes(product, 1, 2))
    identity = jnp.eye(B, dtype=jnp.float32)
    return symmetric + base_diag[:, :, None] * identity


def plant(result, own_key, smallest, largest):
    longest = result.shape.index(max(result.shape))
    spots = []
    for shift in (0, 1):
        where = [jax.random.randint(jax.random.fold_in(own_key, axis), (), 0, length) for axis, length in enumerate(result.shape)]
        where[longest] = (where[longest] + shift) % result.shape[longest]
        spots.append(tuple(where))
    return result.at[spots[0]].set(smallest).at[spots[1]].set(largest)


def steps_of(own_key, shape, shards, smallest, largest):
    def one(axis_at, blocks):
        draws = jax.random.uniform(jax.random.fold_in(jax.random.fold_in(own_key, 6), axis_at), (blocks,), jnp.float32, smallest / len(shards), largest / len(shards))
        return jnp.repeat(jnp.exp(draws), shape[axis_at] // blocks).reshape((-1,) + (1,) * (len(shape) - axis_at - 1))

    level = one(*shards[0])
    for cut in shards[1:]:
        level = level * one(*cut)
    return level


def noise(stream_key, shape, spread, limit, cuts=(), kind=jnp.bfloat16):
    level = steps_of(stream_key, shape, cuts, -0.22, 0.18) if cuts else 1.0
    entries = jax.random.normal(stream_key, shape, jnp.float32) * spread * level
    return jnp.minimum(jnp.maximum(entries, -limit), limit).astype(kind)


def setup_inputs(seed: int = 0, part: int = 0) -> dict:
    arg_keys = jax.random.split(jax.random.key(seed), 9)
    part_splits = jax.random.split(jax.random.fold_in(arg_keys[8], part), 9)
    obs_panel = noise(part_splits[0], (ROWS_ALL, B), (ROWS_TIME // 4) ** -0.5, 0.375, ((0, 16),))
    node_index = plant(jax.random.randint(part_splits[1], (ROWS_ALL,), 0, B), jax.random.fold_in(part_splits[1], 1), 0, B - 1).astype(jnp.int32)
    weight = jnp.clip(jnp.exp(math.log(0.5) - 2.306499 * jax.random.uniform(part_splits[2], (ROWS_ALL,), jnp.float32) ** steps_of(part_splits[2], (ROWS_ALL,), ((0, 16),), -0.2, 0.2)), 0.049804688, 0.5).astype(jnp.bfloat16)
    residual = noise(part_splits[3], (ROWS_ALL,), 1.0, 6.0, ((0, 16),))
    route_time = draw_route_time(jax.random.fold_in(jax.random.fold_in(arg_keys[8], part), 71), part)
    spatial_prec = draw_spatial_prec(jax.random.fold_in(jax.random.fold_in(arg_keys[8], part), 71), part)
    ar_coef = jnp.clip(0.5 + 0.35000002 * jax.random.uniform(part_splits[6], (NT,), jnp.float32) ** steps_of(part_splits[6], (NT,), ((0, 4),), -0.2, 0.2), 0.5, 0.85)
    prior_rhs = noise(part_splits[7], (NT, B), 1.0, 6.0, ((0, 4), (1, 4)), jnp.float32)
    return dict(obs_panel=obs_panel, node_index=node_index, weight=weight, residual=residual, route_time=route_time, spatial_prec=spatial_prec, ar_coef=ar_coef, prior_rhs=prior_rhs)


HIGHEST = lax.Precision.HIGHEST

def eliminate(diag_block, rhs_vec, left_couple, right_couple):
    count = diag_block.shape[0]
    factor = jnp.linalg.cholesky(diag_block)
    stacked = jnp.concatenate([left_couple.T, right_couple, rhs_vec[:, None]], axis=1)
    solved = lax.linalg.triangular_solve(factor, stacked, left_side=True, lower=True)
    left_y = solved[:, :count]
    right_y = solved[:, count:2 * count]
    reduced = solved[:, 2 * count]
    left_b = left_y.astype(jnp.bfloat16)
    right_b = right_y.astype(jnp.bfloat16)
    loss_left = jnp.dot(left_b.T.astype(jnp.float32), left_b.astype(jnp.float32), preferred_element_type=jnp.float32)
    loss_right = jnp.dot(right_b.T.astype(jnp.float32), right_b.astype(jnp.float32), preferred_element_type=jnp.float32)
    fill_new = -jnp.dot(left_b.T.astype(jnp.float32), right_b.astype(jnp.float32), preferred_element_type=jnp.float32)
    up_left = jnp.dot(reduced, left_y, precision=HIGHEST)
    up_right = jnp.dot(reduced, right_y, precision=HIGHEST)
    return (loss_left, loss_right, fill_new, up_left, up_right)

def reference(obs_panel, node_index, weight, residual, route_time, spatial_prec, ar_coef, prior_rhs):
    weighted_res = (weight.astype(jnp.float32) * residual.astype(jnp.float32)).astype(jnp.bfloat16)
    node_hits = (node_index[:, None] == jnp.arange(B, dtype=jnp.int32)[None, :]).astype(jnp.float32)
    design = (obs_panel.astype(jnp.float32) + node_hits).astype(jnp.bfloat16)
    weighted = (weight.astype(jnp.float32)[:, None] * design.astype(jnp.float32)).astype(jnp.bfloat16)
    row_order = jnp.argsort(route_time, stable=True).astype(jnp.int32)
    counts = jnp.sum((route_time[:, None] == jnp.arange(NT, dtype=jnp.int32)[None, :]).astype(jnp.int32), axis=0)
    starts = (jnp.cumsum(counts) - counts).astype(jnp.int32)
    most_rows = SOURCES * CAP
    padding = jnp.zeros((most_rows, B), jnp.bfloat16)
    sorted_design = jnp.concatenate([design[row_order], padding], axis=0)
    sorted_weighted = jnp.concatenate([weighted[row_order], padding], axis=0)
    sorted_res = jnp.concatenate([weighted_res[row_order], jnp.zeros((most_rows,), jnp.bfloat16)], axis=0)

    def per_time(time_step):
        begin = starts[time_step]
        live_rows = (jnp.arange(most_rows, dtype=jnp.int32) < counts[time_step]).astype(jnp.float32)
        rows_design = lax.dynamic_slice_in_dim(sorted_design, begin, most_rows, 0).astype(jnp.float32)
        rows_weighted = lax.dynamic_slice_in_dim(sorted_weighted, begin, most_rows, 0).astype(jnp.float32) * live_rows[:, None]
        rows_res = lax.dynamic_slice_in_dim(sorted_res, begin, most_rows, 0).astype(jnp.float32) * live_rows
        gram_part = jnp.dot(rows_design.T, rows_weighted, precision=HIGHEST)
        grad_part = jnp.dot(rows_res, rows_design, precision=HIGHEST)
        return (gram_part, grad_part)
    grams, grads = lax.map(per_time, jnp.arange(NT, dtype=jnp.int32))
    next_prec = jnp.roll(spatial_prec, -1, axis=0)
    next_coef = jnp.roll(ar_coef, -1)
    diag_one = spatial_prec + (next_coef * next_coef)[:, None, None] * next_prec + grams
    rhs_one = prior_rhs + grads
    couple = -next_coef[:, None, None] * next_prec
    diag_two = [diag_one[step] for step in range(NT)]
    rhs_two = [rhs_one[step] for step in range(NT)]
    fills_one = {}
    for time_step in range(1, NT, 2):
        left_time = time_step - 1
        right_time = (time_step + 1) % NT
        loss_left, loss_right, fill_new, up_left, up_right = eliminate(diag_one[time_step], rhs_one[time_step], couple[left_time], couple[time_step])
        diag_two[left_time] = diag_two[left_time] - loss_left
        diag_two[right_time] = diag_two[right_time] - loss_right
        rhs_two[left_time] = rhs_two[left_time] - up_left
        rhs_two[right_time] = rhs_two[right_time] - up_right
        fills_one[time_step] = fill_new
    diag_three = list(diag_two)
    rhs_three = list(rhs_two)
    fills_two = {}
    for time_step in range(2, NT, 4):
        left_time = time_step - 2
        right_time = (time_step + 2) % NT
        loss_left, loss_right, fill_new, up_left, up_right = eliminate(diag_two[time_step], rhs_two[time_step], fills_one[time_step - 1], fills_one[time_step + 1])
        diag_three[left_time] = diag_three[left_time] - loss_left
        diag_three[right_time] = diag_three[right_time] - loss_right
        rhs_three[left_time] = rhs_three[left_time] - up_left
        rhs_three[right_time] = rhs_three[right_time] - up_right
        fills_two[time_step] = fill_new
    fill_list = []
    for time_step in range(NT):
        if time_step % 2 == 1:
            fill_list.append(fills_one[time_step])
        elif time_step % 4 == 2:
            fill_list.append(fills_two[time_step])
        else:
            fill_list.append(jnp.zeros((B, B), jnp.float32))
    return (jnp.stack(diag_three), jnp.stack(fill_list), jnp.stack(rhs_three))
```

```python
import functools

import jax
import jax.numpy as jnp
from jax import lax
from jax.experimental import pallas as pl
from jax.experimental.pallas import tpu as pltpu
from jax.sharding import PartitionSpec as P

F32 = jnp.float32
BF16 = jnp.bfloat16
NN = (((1,), (0,)), ((), ()))
NT = (((1,), (1,)), ((), ()))
CELLS = ("space", "obs")
GOAL = 2e-4
DOUBLINGS = 12
REFINES = 12


def split(value):
    high = value.astype(BF16)
    return high, (value - high.astype(F32)).astype(BF16)


def mm(left, right, dims=NN):
    return lax.dot_general(left, right, dims, preferred_element_type=F32)


def solve_kernel(tile, diag_ref, rows_ref, left_ref, right_ref, rhs_ref, out_left, out_right, up_ref, ok_ref,
                 dh, dl, x, e, sq, gh, gl, g, res):
    count = diag_ref.shape[0]
    many = rows_ref.shape[0]
    tiles = count // tile

    def strip(i):
        return pl.ds(pl.multiple_of(i * tile, tile), tile)

    def eye(i):
        row = lax.broadcasted_iota(jnp.int32, (tile, count), 0) + i * tile
        col = lax.broadcasted_iota(jnp.int32, (tile, count), 1)
        return (row == col).astype(F32)

    def cut(i, _):
        high, low = split(diag_ref[strip(i), :])
        dh[strip(i), :] = high
        dl[strip(i), :] = low
        return 0

    lax.fori_loop(0, tiles, cut, 0)

    def square(i, most):
        part = mm(dh[strip(i), :], dh[...])
        sq[strip(i), :] = part
        return jnp.maximum(most, jnp.max(jnp.sum(jnp.abs(part), axis=1)))

    most = lax.fori_loop(0, tiles, square, jnp.float32(0.0))
    bound = jnp.sqrt(jnp.full((1, 128), most, F32)) * 1.03
    scale = (1.9 / bound)[:, :1]

    def first(i, total):
        diag = diag_ref[strip(i), :]
        one = eye(i)
        err = one - (2.0 * scale) * diag + (scale * scale) * sq[strip(i), :]
        x[strip(i), :] = scale * (2.0 * one - scale * diag)
        e[0, strip(i), :] = err.astype(BF16)
        return total + jnp.sum(err * err)

    total = lax.fori_loop(0, tiles, first, jnp.float32(0.0))

    def more(state):
        step, total = state
        return (total > 0.5) & (step < DOUBLINGS)

    def double(state):
        step, _ = state
        now = lax.rem(step, 2)

        def body(i, total):
            full = e[now]
            part = x[strip(i), :]
            x[strip(i), :] = part + mm(part.astype(BF16), full)
            err = mm(e[now, strip(i), :], full)
            e[1 - now, strip(i), :] = err.astype(BF16)
            return total + jnp.sum(err * err)

        return step + 1, lax.fori_loop(0, tiles, body, jnp.float32(0.0))

    step, _ = lax.while_loop(more, double, (jnp.int32(0), total))
    last = lax.rem(step, 2)

    def finish(i, _):
        part = x[strip(i), :]
        dl_part = part + mm(part.astype(BF16), e[last])
        sq[strip(i), :] = dl_part
        return 0

    lax.fori_loop(0, tiles, finish, 0)

    def inverse(i, _):
        e[0, strip(i), :] = sq[strip(i), :].astype(BF16)
        return 0

    lax.fori_loop(0, tiles, inverse, 0)
    g[...] = mm(rows_ref[...].astype(BF16), e[0])
    scale_rows = jnp.sum(rows_ref[...] * rows_ref[...], axis=1, keepdims=True) + 1e-30

    def residual():
        high, low = split(g[...])
        gh[...] = high
        gl[...] = low
        rest = rows_ref[...] - (mm(high, dh[...]) + mm(low, dh[...]) + mm(high, dl[...]))
        res[...] = rest.astype(BF16)
        return jnp.max(jnp.sum(rest * rest, axis=1, keepdims=True) / scale_rows)

    def again(state):
        step, size = state
        return (size > GOAL * GOAL) & (step < REFINES)

    def refine(state):
        step, _ = state
        g[...] += mm(res[...], e[0])
        return step + 1, residual()

    _, size = lax.while_loop(again, refine, (jnp.int32(0), residual()))
    ok_ref[0, 0] = jnp.where(size <= GOAL * GOAL, 1, 0).astype(jnp.int32)
    full_left = left_ref[...]
    full_right = right_ref[...]
    out_left[...] = mm(gh[...], full_left, NT) + mm(gl[...], full_left, NT)
    out_right[...] = mm(gh[...], full_right, NT) + mm(gl[...], full_right, NT)
    up_ref[...] = jnp.sum(g[...] * rhs_ref[...], axis=1, keepdims=True)


def solve(diag, rows, full_left, full_right, rhs, counts):
    count = diag.shape[0]
    many = rows.shape[0]
    vmem = pl.BlockSpec(memory_space=pltpu.VMEM)
    tile = 256 if count % 256 == 0 else count
    out_left, out_right, up, ok = pl.pallas_call(
        functools.partial(solve_kernel, tile),
        out_shape=(
            jax.ShapeDtypeStruct((many, count), F32),
            jax.ShapeDtypeStruct((many, count), F32),
            jax.ShapeDtypeStruct((many, 1), F32),
            jax.ShapeDtypeStruct((1, 1), jnp.int32),
        ),
        in_specs=[vmem] * 5,
        out_specs=(vmem, vmem, vmem, pl.BlockSpec(memory_space=pltpu.SMEM)),
        scratch_shapes=[
            pltpu.VMEM((count, count), BF16),
            pltpu.VMEM((count, count), BF16),
            pltpu.VMEM((count, count), F32),
            pltpu.VMEM((2, count, count), BF16),
            pltpu.VMEM((count, count), F32),
            pltpu.VMEM((many, count), BF16),
            pltpu.VMEM((many, count), BF16),
            pltpu.VMEM((many, count), F32),
            pltpu.VMEM((many, count), BF16),
        ],
        compiler_params=pltpu.CompilerParams(vmem_limit_bytes=48 * 1024 * 1024),
    )(diag, rows, full_left, full_right, rhs)

    def direct():
        factor = jnp.linalg.cholesky(diag)
        half = lax.linalg.triangular_solve(factor, rows.T, left_side=True, lower=True)
        g = lax.linalg.triangular_solve(factor, half, left_side=True, lower=True, transpose_a=True).T
        products = [
            lax.dot_general(g, full.astype(F32), NT, precision=lax.Precision.HIGHEST)
            for full in (full_left, full_right)
        ]
        return products[0], products[1], jnp.sum(g * rhs, axis=1, keepdims=True)

    return lax.cond((ok[0, 0] == 1) | ~counts, lambda: (out_left, out_right, up), direct)


def gather(value):
    return lax.all_gather(value, CELLS, axis=0, tiled=True)


def gather_diag(diag_rows, rhs_rows, cell):
    mine, count = diag_rows.shape
    at = (lax.iota(jnp.int32, mine) + cell * mine)[:, None] == lax.iota(jnp.int32, count)[None, :]
    high = diag_rows.astype(BF16)
    rest = jnp.sum(jnp.where(at, diag_rows - high.astype(F32), 0.0), axis=1)
    rhs_high, rhs_low = split(rhs_rows)
    extra = jnp.stack([rest.astype(BF16), rhs_high, rhs_low], axis=1)
    full = gather(jnp.concatenate([high, jnp.pad(extra, ((0, 0), (0, 125)))], axis=1)).astype(F32)
    body = full[:, :count] + full[:, count][:, None] * jnp.eye(count, dtype=F32)
    return body, (full[:, count + 1] + full[:, count + 2])[None, :]


def from_behind(value, axis, steps):
    size = lax.axis_size(axis)
    pairs = [(source, (source + steps) % size) for source in range(size)]
    return lax.ppermute(value, axis, pairs)


def route(obs_panel, node_index, weight, residual, route_time):
    n_times = lax.axis_size("tm")
    rows_dev, count = obs_panel.shape
    capacity = 2 * rows_dev // n_times
    slots = n_times * capacity
    weighted_res = (weight.astype(F32) * residual.astype(F32)).astype(BF16)
    hits = (node_index[:, None] == lax.iota(jnp.int32, count)[None, :]).astype(F32)
    design = (obs_panel.astype(F32) + hits).astype(BF16)
    marks = route_time[:, None] == lax.iota(jnp.int32, n_times)[None, :]
    below = lax.iota(jnp.int32, rows_dev)[:, None] > lax.iota(jnp.int32, rows_dev)[None, :]
    before = mm(below.astype(BF16), marks.astype(BF16))
    rank = jnp.sum(jnp.where(marks, before, 0.0), axis=1).astype(jnp.int32)
    slot = route_time * capacity + rank
    pick = (lax.iota(jnp.int32, slots)[:, None] == slot[None, :]).astype(BF16)
    extra = jnp.pad(jnp.stack([weight, weighted_res], axis=1), ((0, 0), (0, 126)))
    send = mm(pick, jnp.concatenate([design, extra], axis=1)).astype(BF16)
    got = lax.all_to_all(
        send.reshape(n_times, capacity, count + 128), "tm", split_axis=0, concat_axis=0, tiled=True
    ).reshape(slots, count + 128)
    return got[:, :count], got[:, count], got[:, count + 1]


def local(obs_panel, node_index, weight, residual, route_time, spatial_prec, ar_coef, prior_rhs):
    time = lax.axis_index("tm")
    cell = lax.axis_index(CELLS)
    mine = spatial_prec.shape[1]
    own_prec = spatial_prec[0]
    next_prec, next_coef = from_behind((own_prec, ar_coef), "tm", -1)
    own_coef, next_coef = ar_coef[0], next_coef[0]
    left_rows = -own_coef * own_prec
    right_rows = -next_coef * next_prec
    full_left, full_right = gather((left_rows.astype(BF16), right_rows.astype(BF16)))
    design, slot_weight, slot_res = route(obs_panel, node_index, weight, residual, route_time)
    weighted = (slot_weight.astype(F32)[:, None] * design.astype(F32)).astype(BF16)
    gram = mm(design, weighted, (((0,), (0,)), ((), ())))
    grad = mm(design, slot_res[:, None], (((0,), (0,)), ((), ())))[:, 0]
    gram, grad = lax.psum_scatter((gram, grad), CELLS, scatter_dimension=0, tiled=True)
    diag_one = own_prec + next_coef * next_coef * next_prec + gram
    rhs_one = prior_rhs[0] + grad

    odd = time % 2 == 1
    diag_full, rhs_full = gather_diag(diag_one, rhs_one, cell)
    rows = jnp.concatenate([left_rows, right_rows], axis=0)
    by_left, by_right, up = solve(diag_full, rows, full_left, full_right, rhs_full, odd)
    fill_one = -by_right[:mine]
    to_left = jnp.concatenate([by_left[:mine], -by_left[mine:]], axis=0).astype(BF16)
    to_right = jnp.concatenate([by_right[mine:], fill_one], axis=0).astype(BF16)
    from_right, up_right = from_behind((to_left, up[:mine, 0]), "tm", -1)
    from_left, up_left = from_behind((to_right, up[mine:, 0]), "tm", 1)
    from_right, from_left = from_right.astype(F32), from_left.astype(F32)
    diag_two = jnp.where(odd, diag_one, diag_one - from_right[:mine] - from_left[:mine])
    rhs_two = jnp.where(odd, rhs_one, rhs_one - up_right - up_left)

    middle = time % 4 == 2
    diag_full, rhs_full = gather_diag(diag_two, rhs_two, cell)
    rows = jnp.concatenate([from_left[mine:], from_right[mine:]], axis=0)
    full_left, full_right = gather((from_left[mine:].astype(BF16), from_right[mine:].astype(BF16)))
    by_left, by_right, up = solve(diag_full, rows, full_left, full_right, rhs_full, middle)
    fill_two = -by_right[:mine]
    back_right, back_up_right = from_behind((by_left[:mine].astype(BF16), up[:mine, 0]), "tm", -2)
    back_left, back_up_left = from_behind((by_right[mine:].astype(BF16), up[mine:, 0]), "tm", 2)
    survive = time % 4 == 0
    diag_three = jnp.where(survive, diag_two - back_right.astype(F32) - back_left.astype(F32), diag_two)
    rhs_three = jnp.where(survive, rhs_two - back_up_right - back_up_left, rhs_two)
    fill = jnp.where(odd, fill_one, jnp.where(middle, fill_two, 0.0))
    return diag_three[None], fill[None], rhs_three[None]


def solution(mesh):
    rows = ("grp", "tm", "space", "obs")
    blocks = P(("grp", "tm"), CELLS, None)
    vectors = P(("grp", "tm"), CELLS)
    return jax.shard_map(
        local,
        mesh=mesh,
        in_specs=(P(rows, None), P(rows), P(rows), P(rows), P(rows), blocks, P(("grp", "tm")), vectors),
        out_specs=(blocks, blocks, vectors),
        check_vma=False,
    )
```

```python
import functools

import jax
import jax.numpy as jnp
from jax import lax
from jax.experimental import pallas as pl
from jax.experimental.pallas import tpu as pltpu
from jax.sharding import PartitionSpec as P

F32 = jnp.float32
BF16 = jnp.bfloat16
NN = (((1,), (0,)), ((), ()))
NT = (((1,), (1,)), ((), ()))
MESH = pl.DeviceIdType.MESH
WIDE = 128
CELLS = ("space", "obs")
GOAL = 2e-3
DOUBLINGS = 12
REFINES = 6


def split(value):
    high = value.astype(BF16)
    return high, (value - high.astype(F32)).astype(BF16)


def mm(left, right, dims=NN):
    return lax.dot_general(left, right, dims, preferred_element_type=F32)


def mm_exact(left, right):
    return lax.dot_general(left, right, NN, precision=lax.Precision.HIGHEST, preferred_element_type=F32)


def solve_kernel(tile, sizes, active_ref, diag_ref, left_ref, right_ref, lows_ref, scales_ref, rhs_ref,
                 out_left, out_right, up_ref, x, e, sq, g, gh, res):
    count = diag_ref.shape[0]
    many = g.shape[0]
    mine = many // 2
    tiles = count // tile
    cell = lax.axis_index("space") * sizes[2] + lax.axis_index("obs")

    def strip(i):
        return pl.ds(pl.multiple_of(i * tile, tile), tile)

    def eye(i):
        row = lax.broadcasted_iota(jnp.int32, (tile, count), 0) + i * tile
        col = lax.broadcasted_iota(jnp.int32, (tile, count), 1)
        return row == col

    def set_rows():
        at = on_diagonal(mine, count, cell)
        here = pl.ds(pl.multiple_of(cell * mine, 16), mine)
        res[:mine, :] = left_ref[here, :].astype(F32) + jnp.where(at, lows_ref[0:1, :], 0.0)
        res[mine:, :] = right_ref[here, :].astype(F32) + jnp.where(at, lows_ref[8:9, :], 0.0)

    def exact_diag(place):
        def body(i, _):
            place[strip(i), :] = diag_ref[strip(i), :].astype(F32) + jnp.where(eye(i), lows_ref[16:17, :], 0.0)
            return 0

        lax.fori_loop(0, tiles, body, 0)

    def sweeps():
        exact_diag(x)
        lane = lax.broadcasted_iota(jnp.int32, (1, count), 1)

        def sweep(k, _):
            pivot_row = x[pl.ds(k, 1), :]
            inv = 1.0 / jnp.sum(jnp.where(lane == k, pivot_row, 0.0), axis=1, keepdims=True)
            row = pivot_row * inv

            def body(i, _):
                part = x[strip(i), :]
                here = lax.broadcasted_iota(jnp.int32, (tile, 1), 0) + i * tile == k
                col = jnp.sum(jnp.where(lane == k, part, 0.0), axis=1, keepdims=True)
                new = jnp.where(lane == k, col * inv, part - col * row)
                x[strip(i), :] = jnp.where(here, jnp.where(lane == k, -inv, row), new)
                return 0

            return lax.fori_loop(0, tiles, body, 0)

        lax.fori_loop(0, count, sweep, 0)
        x[...] = -x[...]

    @pl.when(active_ref[0] == 1)
    def _():
        set_rows()

        def square(i, most):
            part = mm(diag_ref[strip(i), :], diag_ref[...])
            sq[strip(i), :] = part
            return jnp.maximum(most, jnp.max(jnp.sum(jnp.abs(part), axis=1)))

        most = lax.fori_loop(0, tiles, square, jnp.float32(0.0))
        bound = jnp.sqrt(jnp.full((1, 128), most, F32)) * 1.03
        scale = (1.9 / bound)[:, :1]

        def first(i, total):
            diag = diag_ref[strip(i), :].astype(F32) * scale
            one = jnp.where(eye(i), 1.0, 0.0)
            err = one - 2.0 * diag + (scale * scale) * sq[strip(i), :]
            x[strip(i), :] = scale * (2.0 * one - diag)
            e[0, strip(i), :] = err.astype(BF16)
            return total + jnp.sum(err * err)

        total = lax.fori_loop(0, tiles, first, jnp.float32(0.0))

        def more(state):
            step, total = state
            return (total > 2.0) & (step < DOUBLINGS)

        def double(state):
            step, _ = state
            now = lax.rem(step, 2)

            def body(i, total):
                full = e[now]
                part = x[strip(i), :]
                x[strip(i), :] = part + mm(part.astype(BF16), full)
                err = mm(e[now, strip(i), :], full)
                e[1 - now, strip(i), :] = err.astype(BF16)
                return total + jnp.sum(err * err)

            return step + 1, lax.fori_loop(0, tiles, body, jnp.float32(0.0))

        step, _ = lax.while_loop(more, double, (jnp.int32(0), total))
        last = lax.rem(step, 2)

        def finish(i, _):
            part = x[strip(i), :]
            e[1 - last, strip(i), :] = (part + mm(part.astype(BF16), e[last])).astype(BF16)
            return 0

        lax.fori_loop(0, tiles, finish, 0)
        inverse = 1 - last
        begin = mm(res[...].astype(BF16), e[inverse]).astype(BF16)
        gh[...] = begin
        g[...] = begin.astype(F32)

        def again(state):
            step, size = state
            return jnp.logical_not(size <= GOAL * GOAL) & (step < REFINES)

        def refine(state):
            step, _ = state
            done = gh[...]
            rest = res[...] - mm(done, diag_ref[...]) - done.astype(F32) * lows_ref[16:17, :]
            res[...] = rest
            more = mm(rest.astype(BF16), e[inverse]).astype(BF16)
            gh[...] = more
            more = more.astype(F32)
            value = g[...] + more
            g[...] = value
            norm = jnp.sum(value * value, axis=1, keepdims=True) + 1e-30
            return step + 1, jnp.max(jnp.sum(more * more, axis=1, keepdims=True) / norm)

        _, size = lax.while_loop(again, refine, (jnp.int32(0), jnp.float32(1.0)))

        @pl.when(jnp.logical_not(size <= GOAL * GOAL))
        def _():
            sweeps()
            exact_diag(sq)
            g[...] = jnp.zeros_like(g)

            def improve(_, carry):
                set_rows()
                rest = res[...] - mm_exact(g[...], sq[...])
                g[...] += mm_exact(rest, x[...])
                return carry

            lax.fori_loop(0, 3, improve, 0)

        left_scale, right_scale = scales_ref[0:1, 0:1], scales_ref[1:2, 0:1]
        top = lax.broadcasted_iota(jnp.int32, (many, 1), 0) < mine
        value = g[...] * jnp.where(top, left_scale, right_scale)
        high, low = split(value)
        gh[...] = high
        for out, full, scale, at in ((out_left, left_ref, left_scale, 0), (out_right, right_ref, right_scale, 8)):
            out[...] = (mm(gh[...], full[...], NT) + value * lows_ref[at : at + 1, :]) * scale
        rhs_high, rhs_low = split(rhs_ref[...])
        up_ref[...] = mm(rhs_high, gh[...], NT) + mm(rhs_low, gh[...], NT) + mm(rhs_high, low, NT)


def solve(sizes, active, diag, full_left, full_right, lows, scales, rhs):
    count = diag.shape[0]
    many = 2 * (count // (sizes[1] * sizes[2]))
    vmem = pl.BlockSpec(memory_space=pltpu.VMEM)
    tile = 256 if count % 256 == 0 else count
    return pl.pallas_call(
        functools.partial(solve_kernel, tile, sizes),
        out_shape=(
            jax.ShapeDtypeStruct((many, count), F32),
            jax.ShapeDtypeStruct((many, count), F32),
            jax.ShapeDtypeStruct((8, many), F32),
        ),
        in_specs=[pl.BlockSpec(memory_space=pltpu.SMEM)] + [vmem] * 6,
        out_specs=(vmem, vmem, vmem),
        scratch_shapes=[
            pltpu.VMEM((count, count), F32),
            pltpu.VMEM((2, count, count), BF16),
            pltpu.VMEM((count, count), F32),
            pltpu.VMEM((many, count), F32),
            pltpu.VMEM((many, count), BF16),
            pltpu.VMEM((many, count), F32),
        ],
        compiler_params=pltpu.CompilerParams(vmem_limit_bytes=48 * 1024 * 1024),
    )(active.astype(jnp.int32).reshape(1), diag, full_left, full_right, lows, scales, rhs)


def turn(value, by, size):
    return lax.rem(value + (by + size), size)


def send(source, target, send_sem, recv_sem, device):
    return pltpu.make_async_remote_copy(
        src_ref=source, dst_ref=target, send_sem=send_sem, recv_sem=recv_sem, device_id=device, device_id_type=MESH
    )


def greet(devices):
    barrier = pltpu.get_barrier_semaphore()
    for device in devices:
        pl.semaphore_signal(barrier, inc=1, device_id=device, device_id_type=MESH)
    pl.semaphore_wait(barrier, len(devices))


def cell_peers(sp, ob, n_space, n_obs):
    return [
        {"space": turn(sp, k, n_space), "obs": turn(ob, o, n_obs)}
        for k in range(n_space)
        for o in range(n_obs)
        if k or o
    ]


class Spread:
    def __init__(self, buf, sems, which, sizes):
        self.buf, self.n_space, self.n_obs = buf, *sizes
        self.send_sems, self.recv_sems = (sem.at[which] for sem in sems)
        self.sp, self.ob = lax.axis_index("space"), lax.axis_index("obs")
        self.sent = []

    def block(self, k, o):
        return self.buf.at[turn(self.sp, -k, self.n_space) * self.n_obs + turn(self.ob, -o, self.n_obs)]

    def copy(self, k, o, forward):
        source = self.block(k, 0) if forward else self.block(0, 0)
        device = {"obs": turn(self.ob, o, self.n_obs)} if forward else {"space": turn(self.sp, k, self.n_space)}
        made = send(source, source, self.send_sems.at[k, o], self.recv_sems.at[k, o], device)
        made.start()
        self.sent.append(made)

    def arrived(self, k, o):
        place = self.block(k, o)
        send(place, place, self.send_sems.at[k, o], self.recv_sems.at[k, o], {"obs": self.ob}).wait_recv()

    def start(self):
        for k in range(1, self.n_space):
            self.copy(k, 0, False)
        for o in range(1, self.n_obs):
            self.copy(0, o, True)

    def forward(self):
        for k in range(1, self.n_space):
            self.arrived(k, 0)
            for o in range(1, self.n_obs):
                self.copy(k, o, True)

    def finish(self):
        for k in range(self.n_space):
            for o in range(1, self.n_obs):
                self.arrived(k, o)
        for made in self.sent:
            made.wait_send()


def on_diagonal(mine, count, cell):
    row = lax.broadcasted_iota(jnp.int32, (mine, count), 0) + cell * mine
    return row == lax.broadcasted_iota(jnp.int32, (mine, count), 1)


def pack(value, place, at, extra):
    mine, count = value.shape
    high = value.astype(BF16)
    rest = jnp.sum(jnp.where(at, value - high.astype(F32), 0.0), axis=1, keepdims=True)
    lane = lax.broadcasted_iota(jnp.int32, (mine, WIDE), 1)
    beside = jnp.where(lane == 0, rest, 0.0)
    for index, column in enumerate(extra):
        beside = jnp.where(lane == index + 1, column, beside)
    place[:, :count] = high
    place[:, count:] = beside.astype(BF16)


def unpack(place, at):
    count = at.shape[1]
    rest = place[:, count : count + 1].astype(F32)
    low = jnp.where(at, rest, 0.0)
    return place[:, :count].astype(F32) + low, low


def assemble_kernel(sizes, send_ref, prec_ref, coef_ref, vec_ref,
                    diag_rows, diag_full, own_out, next_out, lows_out, scales_out, rhs_out,
                    slabs, arriving, design, weighted, part, part_high, from_mate, half, from_space,
                    own_buf, next_buf, diag_buf, vec_buf,
                    slab_send, slab_recv, prec_sems, mate_send, mate_recv, half_send, half_recv, all_send, all_recv):
    n_times, n_space, n_obs = sizes
    mine, count = prec_ref.shape
    capacity = send_ref.shape[1]
    tm, sp, ob = lax.axis_index("tm"), lax.axis_index("space"), lax.axis_index("obs")
    cell = sp * n_obs + ob
    cells = n_space * n_obs
    at = on_diagonal(mine, count, cell)
    greet([{"tm": turn(tm, k, n_times)} for k in range(1, n_times)] + cell_peers(sp, ob, n_space, n_obs))

    moves = []

    def slab(k):
        there = turn(tm, k, n_times)
        return send(send_ref.at[there], slabs.at[tm], slab_send.at[k], slab_recv.at[k], {"tm": there})

    early, late = list(range(1, n_times, 2)), list(range(2, n_times, 2))
    for parity, first in ((0, early), (1, late)):
        @pl.when(lax.rem(tm, 2) == parity)
        def _():
            for k in first:
                slab(k).start()

    coef = coef_ref[0:1, 0:1]
    coef_high = coef.astype(BF16).astype(F32)
    coef_mid = (coef - coef_high).astype(BF16).astype(F32)
    pack(prec_ref[...], own_buf.at[cell], at, (coef_high, coef_mid, coef - coef_high - coef_mid))
    prec_move = send(own_buf.at[cell], arriving, prec_sems.at[0], prec_sems.at[1], {"tm": turn(tm, -1, n_times)})
    even = lax.rem(tm, 2) == 0

    @pl.when(even)
    def _():
        prec_move.start()

    both = (all_send, all_recv)
    spreads = [Spread(buf, both, i, (n_space, n_obs)) for i, buf in enumerate((own_buf, next_buf, diag_buf, vec_buf))]
    own_spread, next_spread, diag_spread, vec_spread = spreads
    own_spread.start()
    slabs[tm] = send_ref[tm]
    for parity, first, second in ((0, early, late), (1, late, early)):
        @pl.when(lax.rem(tm, 2) == parity)
        def _():
            for k in first:
                slab(k).wait_send()
            if parity == 1:
                prec_move.start()
            for k in second:
                slab(k).start()

    prec_move.wait_recv()
    next_buf[cell] = arriving[...]
    next_spread.start()
    own_spread.forward()
    for k in range(1, n_times):
        place = slabs.at[turn(tm, -k, n_times)]
        send(place, place, slab_send.at[k], slab_recv.at[k], {"tm": tm}).wait_recv()

    grad = jnp.zeros((1, count), F32)
    for t in range(n_times):
        held = slabs[t]
        rows = held[:, :count].astype(F32)
        design[:, t * capacity : (t + 1) * capacity] = rows.T.astype(BF16)
        weighted[t * capacity : (t + 1) * capacity, :] = (held[:, count : count + 1].astype(F32) * rows).astype(BF16)
        grad = grad + jnp.sum(held[:, count + 1 : count + 2].astype(F32) * rows, axis=0, keepdims=True)
    vec_buf[cell] = vec_ref[...] + jnp.broadcast_to(grad, (8, count))
    vec_spread.start()
    for o in range(n_obs):
        for s in range(n_space):
            first = (s * n_obs + o) * mine
            value = mm(design[first : first + mine, :], weighted[...])
            part[o, s] = value
            part_high[o, s] = value.astype(BF16)
    for o in range(1, n_obs):
        mate = turn(ob, o, n_obs)
        move = send(part_high.at[mate], from_mate.at[o], mate_send.at[o], mate_recv.at[o], {"obs": mate})
        move.start()
        moves.append(move)
    next_spread.forward()
    vec_spread.forward()
    for o in range(1, n_obs):
        place = from_mate.at[o]
        send(place, place, mate_send.at[o], mate_recv.at[o], {"obs": ob}).wait_recv()

    def chip_sum(s):
        value = part[ob, s]
        for o in range(1, n_obs):
            value = value + from_mate[o, s].astype(F32)
        return value

    for k in range(1, n_space):
        there = turn(sp, k, n_space)
        half[k] = chip_sum(there).astype(BF16)
        move = send(half.at[k], from_space.at[k], half_send.at[k], half_recv.at[k], {"space": there})
        move.start()
        moves.append(move)
    gram = chip_sum(sp)
    next_rows, _ = unpack(next_buf.at[cell], at)
    three = next_buf[cell, :, count + 1 : count + 4].astype(F32)
    next_coef = jnp.sum(three, axis=1, keepdims=True)
    base = prec_ref[...] + next_coef * next_coef * next_rows + gram
    for k in range(1, n_space):
        place = from_space.at[k]
        send(place, place, half_send.at[k], half_recv.at[k], {"space": sp}).wait_recv()
        base = base + from_space[k].astype(F32)
    diag_rows[...] = base
    pack(base, diag_buf.at[cell], at, ())
    diag_spread.start()
    scales_out[0:1, :] = jnp.broadcast_to(-coef, (1, WIDE))
    scales_out[1:2, :] = jnp.broadcast_to(-next_coef[0:1, :], (1, WIDE))
    scales_out[2:8, :] = jnp.zeros((6, WIDE), F32)
    own_spread.finish()
    next_spread.finish()
    vec_spread.finish()
    total = vec_buf[0]
    for c in range(1, cells):
        total = total + vec_buf[c]
    rhs_out[...] = total
    def emit(at_row, buf, out):
        low_sum = jnp.zeros((1, count), F32)
        for c in range(cells):
            _, low = unpack(buf.at[c], on_diagonal(mine, count, c))
            low_sum = low_sum + jnp.sum(low, axis=0, keepdims=True)
            out[c * mine : (c + 1) * mine, :] = buf[c, :, :count]
        lows_out[at_row : at_row + 8, :] = jnp.broadcast_to(low_sum, (8, count))

    emit(0, own_buf, own_out)
    emit(8, next_buf, next_out)
    diag_spread.forward()
    diag_spread.finish()
    emit(16, diag_buf, diag_full)
    prec_move.wait_send()
    for parity, second in ((0, late), (1, early)):
        @pl.when(lax.rem(tm, 2) == parity)
        def _():
            for k in second:
                slab(k).wait_send()

    for move in moves:
        move.wait_send()


def assemble(sizes, sending, prec, coef, vec):
    n_times, n_space, n_obs = sizes
    mine, count = prec.shape
    capacity = sending.shape[1]
    cells = n_space * n_obs
    slots = n_times * capacity
    vmem = pl.BlockSpec(memory_space=pltpu.VMEM)
    dma = pltpu.SemaphoreType.DMA
    wide = (cells, mine, count + WIDE)
    return pl.pallas_call(
        functools.partial(assemble_kernel, sizes),
        out_shape=(
            jax.ShapeDtypeStruct((mine, count), F32),
            jax.ShapeDtypeStruct((count, count), BF16),
            jax.ShapeDtypeStruct((count, count), BF16),
            jax.ShapeDtypeStruct((count, count), BF16),
            jax.ShapeDtypeStruct((24, count), F32),
            jax.ShapeDtypeStruct((8, WIDE), F32),
            jax.ShapeDtypeStruct((8, count), F32),
        ),
        in_specs=[vmem] * 4,
        out_specs=(vmem,) * 7,
        scratch_shapes=[
            pltpu.VMEM((n_times, capacity, count + WIDE), BF16),
            pltpu.VMEM((mine, count + WIDE), BF16),
            pltpu.VMEM((count, slots), BF16),
            pltpu.VMEM((slots, count), BF16),
            pltpu.VMEM((n_obs, n_space, mine, count), F32),
            pltpu.VMEM((n_obs, n_space, mine, count), BF16),
            pltpu.VMEM((n_obs, n_space, mine, count), BF16),
            pltpu.VMEM((n_space, mine, count), BF16),
            pltpu.VMEM((n_space, mine, count), BF16),
            pltpu.VMEM(wide, BF16),
            pltpu.VMEM(wide, BF16),
            pltpu.VMEM(wide, BF16),
            pltpu.VMEM((cells, 8, count), F32),
            dma((n_times,)),
            dma((n_times,)),
            dma((2,)),
            dma((n_obs,)),
            dma((n_obs,)),
            dma((n_space,)),
            dma((n_space,)),
            dma((4, n_space, n_obs)),
            dma((4, n_space, n_obs)),
        ],
        compiler_params=pltpu.CompilerParams(
            collective_id=0, has_side_effects=True, vmem_limit_bytes=48 * 1024 * 1024
        ),
    )(sending, prec, coef, vec)


def reduce_kernel(sizes, by_left, by_right, up_left, up_right, diag_ref, rhs_ref,
                  diag_rows, diag_full, left_out, right_out, lows_out, rhs_out,
                  to_left, to_right, loss_left, loss_right, in_up_left, in_up_right,
                  left_buf, right_buf, diag_buf, vec_buf,
                  send_sems, recv_sems, all_send, all_recv):
    n_times, n_space, n_obs = sizes
    mine, count = diag_ref.shape
    tm, sp, ob = lax.axis_index("tm"), lax.axis_index("space"), lax.axis_index("obs")
    cell = sp * n_obs + ob
    cells = n_space * n_obs
    left, right = {"tm": turn(tm, -1, n_times)}, {"tm": turn(tm, 1, n_times)}
    greet([left, right] + cell_peers(sp, ob, n_space, n_obs))
    kind = lax.rem(tm, 4)

    def fill_copy(is_left):
        buf, source = (right_buf, to_left) if is_left else (left_buf, to_right)
        which = 3 if is_left else 0
        return send(source.at[1], buf.at[cell], send_sems.at[which], recv_sems.at[which], left if is_left else right)

    def loss_copy(is_left):
        buf, source = (loss_right, to_left) if is_left else (loss_left, to_right)
        which = 4 if is_left else 1
        return send(source.at[0], buf, send_sems.at[which], recv_sems.at[which], left if is_left else right)

    def up_copy(is_left):
        buf, source = (in_up_right, up_left) if is_left else (in_up_left, up_right)
        which = 5 if is_left else 2
        return send(source, buf, send_sems.at[which], recv_sems.at[which], left if is_left else right)

    for middle_left in (False, True):
        @pl.when(kind == (3 if middle_left else 1))
        def _():
            near = to_left if middle_left else to_right
            if middle_left:
                near[1] = (-by_left[mine:, :]).astype(BF16)
            else:
                near[1] = (-by_right[:mine, :]).astype(BF16)
            first = fill_copy(middle_left)
            first.start()
            near[0] = (by_left[:mine, :] if middle_left else by_right[mine:, :]).astype(BF16)
            second = loss_copy(middle_left)
            second.start()
            third = up_copy(middle_left)
            third.start()
            far = to_right if middle_left else to_left
            far[0] = (by_right[mine:, :] if middle_left else by_left[:mine, :]).astype(BF16)
            first.wait_send()
            second.wait_send()
            others = [loss_copy(not middle_left), up_copy(not middle_left)]
            for move in others:
                move.start()
            for move in [third] + others:
                move.wait_send()

    @pl.when(kind != 2)
    def _():
        rhs_out[...] = rhs_ref[...]

    @pl.when(kind % 2 == 1)
    def _():
        diag_rows[...] = diag_ref[...]

    @pl.when(kind == 0)
    def _():
        for is_left in (False, True):
            loss_copy(is_left).wait_recv()
            up_copy(is_left).wait_recv()
        diag_rows[...] = diag_ref[...] - loss_left[...].astype(F32) - loss_right[...].astype(F32)
        rhs_out[...] = rhs_ref[...] - in_up_left[...] - in_up_right[...]

    @pl.when(kind == 2)
    def _():
        both = (all_send, all_recv)
        spreads = [
            Spread(buf, both, i, (n_space, n_obs)) for i, buf in enumerate((left_buf, right_buf, diag_buf, vec_buf))
        ]
        fill_copy(False).wait_recv()
        spreads[0].start()
        fill_copy(True).wait_recv()
        spreads[1].start()
        loss_copy(False).wait_recv()
        loss_copy(True).wait_recv()
        base = diag_ref[...] - loss_left[...].astype(F32) - loss_right[...].astype(F32)
        diag_rows[...] = base
        pack(base, diag_buf.at[cell], on_diagonal(mine, count, cell), ())
        spreads[2].start()
        up_copy(False).wait_recv()
        up_copy(True).wait_recv()
        vec_buf[cell] = in_up_left[...] + in_up_right[...]
        spreads[3].start()
        for spread in spreads:
            spread.forward()
        for spread in spreads:
            spread.finish()
        total = rhs_ref[...]
        low_sum = jnp.zeros((1, count), F32)
        for c in range(cells):
            total = total - vec_buf[c]
            left_out[c * mine : (c + 1) * mine, :] = left_buf[c]
            right_out[c * mine : (c + 1) * mine, :] = right_buf[c]
            _, low = unpack(diag_buf.at[c], on_diagonal(mine, count, c))
            low_sum = low_sum + jnp.sum(low, axis=0, keepdims=True)
            diag_full[c * mine : (c + 1) * mine, :] = diag_buf[c, :, :count]
        lows_out[:16, :] = jnp.zeros((16, count), F32)
        lows_out[16:, :] = jnp.broadcast_to(low_sum, (8, count))
        rhs_out[...] = total


def reduce_level(sizes, by_left, by_right, up_left, up_right, diag, rhs):
    n_times, n_space, n_obs = sizes
    mine, count = diag.shape
    cells = n_space * n_obs
    vmem = pl.BlockSpec(memory_space=pltpu.VMEM)
    dma = pltpu.SemaphoreType.DMA
    return pl.pallas_call(
        functools.partial(reduce_kernel, sizes),
        out_shape=(
            jax.ShapeDtypeStruct((mine, count), F32),
            jax.ShapeDtypeStruct((count, count), BF16),
            jax.ShapeDtypeStruct((count, count), BF16),
            jax.ShapeDtypeStruct((count, count), BF16),
            jax.ShapeDtypeStruct((24, count), F32),
            jax.ShapeDtypeStruct((8, count), F32),
        ),
        in_specs=[vmem] * 6,
        out_specs=(vmem,) * 6,
        scratch_shapes=[
            pltpu.VMEM((2, mine, count), BF16),
            pltpu.VMEM((2, mine, count), BF16),
            pltpu.VMEM((mine, count), BF16),
            pltpu.VMEM((mine, count), BF16),
            pltpu.VMEM((8, count), F32),
            pltpu.VMEM((8, count), F32),
            pltpu.VMEM((cells, mine, count), BF16),
            pltpu.VMEM((cells, mine, count), BF16),
            pltpu.VMEM((cells, mine, count + WIDE), BF16),
            pltpu.VMEM((cells, 8, count), F32),
            dma((6,)),
            dma((6,)),
            dma((4, n_space, n_obs)),
            dma((4, n_space, n_obs)),
        ],
        compiler_params=pltpu.CompilerParams(
            collective_id=1, has_side_effects=True, vmem_limit_bytes=48 * 1024 * 1024
        ),
    )(by_left, by_right, up_left, up_right, diag, rhs)


def last_kernel(n_times, by_left, by_right, up_left, up_right, loss_out, up_out,
                loss_send, loss_recv, up_send, up_recv, sems):
    mine = loss_out.shape[0]
    tm = lax.axis_index("tm")
    ways = [-2] if n_times == 4 else [-2, 2]
    greet([{"tm": turn(tm, way, n_times)} for way in ways])
    kind = lax.rem(tm, 4)

    def copies(i, way):
        device = {"tm": turn(tm, way, n_times)}
        return [
            send(loss_send.at[i], loss_recv.at[i], sems.at[0, i], sems.at[1, i], device),
            send(up_send.at[i], up_recv.at[i], sems.at[2, i], sems.at[3, i], device),
        ]

    @pl.when(kind == 2)
    def _():
        if n_times == 4:
            loss_send[0] = (by_left[:mine, :] + by_right[mine:, :]).astype(BF16)
            up_send[0] = up_left[...] + up_right[...]
        else:
            loss_send[0] = by_left[:mine, :].astype(BF16)
            loss_send[1] = by_right[mine:, :].astype(BF16)
            up_send[0] = up_left[...]
            up_send[1] = up_right[...]
        moves = [move for i, way in enumerate(ways) for move in copies(i, way)]
        for move in moves:
            move.start()
        for move in moves:
            move.wait_send()

    @pl.when(kind == 0)
    def _():
        for i, way in enumerate(ways):
            for move in copies(i, way):
                move.wait_recv()
        loss = loss_recv[0].astype(F32)
        up = up_recv[0]
        for i in range(1, len(ways)):
            loss = loss + loss_recv[i].astype(F32)
            up = up + up_recv[i]
        loss_out[...] = loss
        up_out[...] = up

    @pl.when(kind != 0)
    def _():
        loss_out[...] = jnp.zeros_like(loss_out)
        up_out[...] = jnp.zeros_like(up_out)


def last_level(n_times, by_left, by_right, up_left, up_right):
    many, count = by_left.shape
    mine = many // 2
    ways = 1 if n_times == 4 else 2
    vmem = pl.BlockSpec(memory_space=pltpu.VMEM)
    return pl.pallas_call(
        functools.partial(last_kernel, n_times),
        out_shape=(jax.ShapeDtypeStruct((mine, count), F32), jax.ShapeDtypeStruct((8, count), F32)),
        in_specs=[vmem] * 4,
        out_specs=(vmem, vmem),
        scratch_shapes=[
            pltpu.VMEM((ways, mine, count), BF16),
            pltpu.VMEM((ways, mine, count), BF16),
            pltpu.VMEM((ways, 8, count), F32),
            pltpu.VMEM((ways, 8, count), F32),
            pltpu.SemaphoreType.DMA((4, ways)),
        ],
        compiler_params=pltpu.CompilerParams(
            collective_id=2, has_side_effects=True, vmem_limit_bytes=32 * 1024 * 1024
        ),
    )(by_left, by_right, up_left, up_right)


def route(obs_panel, node_index, weight, residual, route_time, n_times):
    rows_dev, count = obs_panel.shape
    capacity = 2 * rows_dev // n_times
    slots = n_times * capacity
    weighted_res = (weight.astype(F32) * residual.astype(F32)).astype(BF16)
    hits = (node_index[:, None] == lax.iota(jnp.int32, count)[None, :]).astype(F32)
    design = (obs_panel.astype(F32) + hits).astype(BF16)
    marks = route_time[:, None] == lax.iota(jnp.int32, n_times)[None, :]
    below = lax.iota(jnp.int32, rows_dev)[:, None] > lax.iota(jnp.int32, rows_dev)[None, :]
    before = mm(below.astype(BF16), marks.astype(BF16))
    rank = jnp.sum(jnp.where(marks, before, 0.0), axis=1).astype(jnp.int32)
    slot = route_time * capacity + rank
    pick = (lax.iota(jnp.int32, slots)[:, None] == slot[None, :]).astype(BF16)
    extra = jnp.pad(jnp.stack([weight, weighted_res], axis=1), ((0, 0), (0, WIDE - 2)))
    sending = mm(pick, jnp.concatenate([design, extra], axis=1)).astype(BF16)
    return sending.reshape(n_times, capacity, count + WIDE)


def local(sizes, obs_panel, node_index, weight, residual, route_time, spatial_prec, ar_coef, prior_rhs):
    n_times, n_space, n_obs = sizes
    time = lax.axis_index("tm")
    cell = lax.axis_index("space") * n_obs + lax.axis_index("obs")
    _, mine, count = spatial_prec.shape

    def placed(row):
        full = lax.dynamic_update_slice(jnp.zeros((1, count), F32), row, (0, cell * mine))
        return jnp.broadcast_to(full, (8, count))

    def mine_of(full):
        return lax.dynamic_slice(full, (0, cell * mine), (1, mine))[0]

    odd = time % 2 == 1
    middle = time % 4 == 2
    sending = route(obs_panel, node_index, weight, residual, route_time, n_times)
    coef = jnp.broadcast_to(ar_coef[:, None], (8, WIDE))
    diag_one, diag_full, full_left, full_right, lows, scales, rhs_one = assemble(
        sizes, sending, spatial_prec[0], coef, placed(prior_rhs)
    )
    by_left, by_right, up = solve(sizes, odd, diag_full, full_left, full_right, lows, scales, rhs_one)
    fill_one = -by_right[:mine]
    diag_two, diag_full, full_left, full_right, lows, rhs_two = reduce_level(
        sizes, by_left, by_right, placed(up[:1, :mine]), placed(up[:1, mine:]), diag_one, rhs_one
    )
    by_left, by_right, up = solve(
        sizes, middle, diag_full, full_left, full_right, lows, jnp.ones_like(scales), rhs_two
    )
    fill_two = -by_right[:mine]
    loss, back = last_level(n_times, by_left, by_right, placed(up[:1, :mine]), placed(up[:1, mine:]))
    fill = jnp.where(odd, fill_one, jnp.where(middle, fill_two, 0.0))
    return (diag_two - loss)[None], fill[None], (mine_of(rhs_two) - mine_of(back))[None]


def solution(mesh):
    rows = ("grp", "tm", "space", "obs")
    blocks = P(("grp", "tm"), CELLS, None)
    vectors = P(("grp", "tm"), CELLS)
    sizes = tuple(mesh.shape[name] for name in ("tm", "space", "obs"))
    return jax.shard_map(
        functools.partial(local, sizes),
        mesh=mesh,
        in_specs=(P(rows, None), P(rows), P(rows), P(rows), P(rows), blocks, P(("grp", "tm")), vectors),
        out_specs=(blocks, blocks, vectors),
        check_vma=False,
    )
```

```python
import functools

import jax
import jax.numpy as jnp
from jax import lax
from jax.experimental import pallas as pl
from jax.experimental.pallas import tpu as pltpu
from jax.sharding import PartitionSpec as P

F32 = jnp.float32
BF16 = jnp.bfloat16
NN = (((1,), (0,)), ((), ()))
NT = (((1,), (1,)), ((), ()))
MESH = pl.DeviceIdType.MESH
WIDE = 128
CELLS = ("space", "obs")
GOAL = 2e-3
DOUBLINGS = 12
REFINES = 6


def split(value):
    high = value.astype(BF16)
    return high, (value - high.astype(F32)).astype(BF16)


def mm(left, right, dims=NN):
    return lax.dot_general(left, right, dims, preferred_element_type=F32)


def mm_exact(left, right):
    return lax.dot_general(left, right, NN, precision=lax.Precision.HIGHEST, preferred_element_type=F32)


def solve_kernel(tile, sizes, active_ref, diag_ref, left_ref, right_ref, lows_ref, scales_ref, rhs_ref,
                 out_left, out_right, up_ref, x, e, sq, g, gh, res):
    count = diag_ref.shape[0]
    many = g.shape[0]
    mine = many // 2
    tiles = count // tile
    cell = lax.axis_index("space") * sizes[2] + lax.axis_index("obs")

    def strip(i):
        return pl.ds(pl.multiple_of(i * tile, tile), tile)

    def eye(i):
        row = lax.broadcasted_iota(jnp.int32, (tile, count), 0) + i * tile
        col = lax.broadcasted_iota(jnp.int32, (tile, count), 1)
        return row == col

    def set_rows():
        at = on_diagonal(mine, count, cell)
        here = pl.ds(pl.multiple_of(cell * mine, 16), mine)
        res[:mine, :] = left_ref[here, :].astype(F32) + jnp.where(at, lows_ref[0:1, :], 0.0)
        res[mine:, :] = right_ref[here, :].astype(F32) + jnp.where(at, lows_ref[8:9, :], 0.0)

    def exact_diag(place):
        def body(i, _):
            place[strip(i), :] = diag_ref[strip(i), :].astype(F32) + jnp.where(eye(i), lows_ref[16:17, :], 0.0)
            return 0

        lax.fori_loop(0, tiles, body, 0)

    def sweeps():
        exact_diag(x)
        lane = lax.broadcasted_iota(jnp.int32, (1, count), 1)

        def sweep(k, _):
            pivot_row = x[pl.ds(k, 1), :]
            inv = 1.0 / jnp.sum(jnp.where(lane == k, pivot_row, 0.0), axis=1, keepdims=True)
            row = pivot_row * inv

            def body(i, _):
                part = x[strip(i), :]
                here = lax.broadcasted_iota(jnp.int32, (tile, 1), 0) + i * tile == k
                col = jnp.sum(jnp.where(lane == k, part, 0.0), axis=1, keepdims=True)
                new = jnp.where(lane == k, col * inv, part - col * row)
                x[strip(i), :] = jnp.where(here, jnp.where(lane == k, -inv, row), new)
                return 0

            return lax.fori_loop(0, tiles, body, 0)

        lax.fori_loop(0, count, sweep, 0)
        x[...] = -x[...]

    @pl.when(active_ref[0] == 1)
    def _():
        set_rows()

        def square(i, most):
            part = mm(diag_ref[...], diag_ref[:, strip(i)])
            sq[:, strip(i)] = part
            return jnp.maximum(most, jnp.max(jnp.sum(jnp.abs(part), axis=0)))

        most = lax.fori_loop(0, tiles, square, jnp.float32(0.0))
        bound = jnp.sqrt(jnp.full((1, 128), most, F32)) * 1.03
        scale = (1.9 / bound)[:, :1]

        def first(i, total):
            diag = diag_ref[strip(i), :].astype(F32) * scale
            one = jnp.where(eye(i), 1.0, 0.0)
            err = one - 2.0 * diag + (scale * scale) * sq[strip(i), :]
            x[strip(i), :] = scale * (2.0 * one - diag)
            e[0, strip(i), :] = err.astype(BF16)
            return total + jnp.sum(err * err)

        total = lax.fori_loop(0, tiles, first, jnp.float32(0.0))

        def more(state):
            step, total = state
            return (total > 2.0) & (step < DOUBLINGS)

        def double(state):
            step, _ = state
            now = lax.rem(step, 2)

            def body(i, total):
                part = x[:, strip(i)]
                x[:, strip(i)] = part + mm(e[now], part.astype(BF16))
                err = mm(e[now], e[now, :, strip(i)])
                e[1 - now, :, strip(i)] = err.astype(BF16)
                return total + jnp.sum(err * err)

            return step + 1, lax.fori_loop(0, tiles, body, jnp.float32(0.0))

        step, _ = lax.while_loop(more, double, (jnp.int32(0), total))
        last = lax.rem(step, 2)

        def finish(i, _):
            part = x[:, strip(i)]
            e[1 - last, :, strip(i)] = (part + mm(e[last], part.astype(BF16))).astype(BF16)
            return 0

        lax.fori_loop(0, tiles, finish, 0)
        inverse = 1 - last
        begin = mm(res[...].astype(BF16), e[inverse]).astype(BF16)
        gh[...] = begin
        g[...] = begin.astype(F32)

        def again(state):
            step, size = state
            return jnp.logical_not(size <= GOAL * GOAL) & (step < REFINES)

        def refine(state):
            step, _ = state
            done = gh[...]
            rest = res[...] - mm(done, diag_ref[...]) - done.astype(F32) * lows_ref[16:17, :]
            res[...] = rest
            more = mm(rest.astype(BF16), e[inverse]).astype(BF16)
            gh[...] = more
            more = more.astype(F32)
            value = g[...] + more
            g[...] = value
            norm = jnp.sum(value * value, axis=1, keepdims=True) + 1e-30
            return step + 1, jnp.max(jnp.sum(more * more, axis=1, keepdims=True) / norm)

        _, size = lax.while_loop(again, refine, (jnp.int32(0), jnp.float32(1.0)))

        @pl.when(jnp.logical_not(size <= GOAL * GOAL))
        def _():
            sweeps()
            exact_diag(sq)
            g[...] = jnp.zeros_like(g)

            def improve(_, carry):
                set_rows()
                rest = res[...] - mm_exact(g[...], sq[...])
                g[...] += mm_exact(rest, x[...])
                return carry

            lax.fori_loop(0, 3, improve, 0)

        left_scale, right_scale = scales_ref[0:1, 0:1], scales_ref[1:2, 0:1]
        top = lax.broadcasted_iota(jnp.int32, (many, 1), 0) < mine
        value = g[...] * jnp.where(top, left_scale, right_scale)
        high, low = split(value)
        gh[...] = high
        for out, full, scale, at in ((out_left, left_ref, left_scale, 0), (out_right, right_ref, right_scale, 8)):
            out[...] = (mm(gh[...], full[...], NT) + value * lows_ref[at : at + 1, :]) * scale
        rhs_high, rhs_low = split(rhs_ref[...])
        up_ref[...] = mm(rhs_high, gh[...], NT) + mm(rhs_low, gh[...], NT) + mm(rhs_high, low, NT)


def solve(sizes, active, diag, full_left, full_right, lows, scales, rhs):
    count = diag.shape[0]
    many = 2 * (count // (sizes[1] * sizes[2]))
    vmem = pl.BlockSpec(memory_space=pltpu.VMEM)
    tile = 256 if count % 256 == 0 else count
    return pl.pallas_call(
        functools.partial(solve_kernel, tile, sizes),
        out_shape=(
            jax.ShapeDtypeStruct((many, count), F32),
            jax.ShapeDtypeStruct((many, count), F32),
            jax.ShapeDtypeStruct((8, many), F32),
        ),
        in_specs=[pl.BlockSpec(memory_space=pltpu.SMEM)] + [vmem] * 6,
        out_specs=(vmem, vmem, vmem),
        scratch_shapes=[
            pltpu.VMEM((count, count), F32),
            pltpu.VMEM((2, count, count), BF16),
            pltpu.VMEM((count, count), F32),
            pltpu.VMEM((many, count), F32),
            pltpu.VMEM((many, count), BF16),
            pltpu.VMEM((many, count), F32),
        ],
        compiler_params=pltpu.CompilerParams(vmem_limit_bytes=28 * 1024 * 1024),
    )(active.astype(jnp.int32).reshape(1), diag, full_left, full_right, lows, scales, rhs)


def turn(value, by, size):
    return lax.rem(value + (by + size), size)


def send(source, target, send_sem, recv_sem, device):
    return pltpu.make_async_remote_copy(
        src_ref=source, dst_ref=target, send_sem=send_sem, recv_sem=recv_sem, device_id=device, device_id_type=MESH
    )


def greet(devices):
    barrier = pltpu.get_barrier_semaphore()
    for device in devices:
        pl.semaphore_signal(barrier, inc=1, device_id=device, device_id_type=MESH)
    pl.semaphore_wait(barrier, len(devices))


def cell_peers(sp, ob, n_space, n_obs):
    return [
        {"space": turn(sp, k, n_space), "obs": turn(ob, o, n_obs)}
        for k in range(n_space)
        for o in range(n_obs)
        if k or o
    ]


class Spread:
    def __init__(self, buf, sems, which, sizes):
        self.buf, self.n_space, self.n_obs = buf, *sizes
        self.send_sems, self.recv_sems = (sem.at[which] for sem in sems)
        self.sp, self.ob = lax.axis_index("space"), lax.axis_index("obs")
        self.sent = []

    def block(self, k, o):
        return self.buf.at[turn(self.sp, -k, self.n_space) * self.n_obs + turn(self.ob, -o, self.n_obs)]

    def copy(self, k, o, forward):
        source = self.block(k, 0) if forward else self.block(0, 0)
        device = {"obs": turn(self.ob, o, self.n_obs)} if forward else {"space": turn(self.sp, k, self.n_space)}
        made = send(source, source, self.send_sems.at[k, o], self.recv_sems.at[k, o], device)
        made.start()
        self.sent.append(made)

    def arrived(self, k, o):
        place = self.block(k, o)
        send(place, place, self.send_sems.at[k, o], self.recv_sems.at[k, o], {"obs": self.ob}).wait_recv()

    def start(self):
        for k in range(1, self.n_space):
            self.copy(k, 0, False)
        for o in range(1, self.n_obs):
            self.copy(0, o, True)

    def forward(self):
        for k in range(1, self.n_space):
            self.arrived(k, 0)
            for o in range(1, self.n_obs):
                self.copy(k, o, True)

    def finish(self):
        for k in range(self.n_space):
            for o in range(1, self.n_obs):
                self.arrived(k, o)
        for made in self.sent:
            made.wait_send()


def on_diagonal(mine, count, cell):
    row = lax.broadcasted_iota(jnp.int32, (mine, count), 0) + cell * mine
    return row == lax.broadcasted_iota(jnp.int32, (mine, count), 1)


def pack(value, place, at, extra):
    mine, count = value.shape
    high = value.astype(BF16)
    rest = jnp.sum(jnp.where(at, value - high.astype(F32), 0.0), axis=1, keepdims=True)
    lane = lax.broadcasted_iota(jnp.int32, (mine, WIDE), 1)
    beside = jnp.where(lane == 0, rest, 0.0)
    for index, column in enumerate(extra):
        beside = jnp.where(lane == index + 1, column, beside)
    place[:, :count] = high
    place[:, count:] = beside.astype(BF16)


def unpack(place, at):
    count = at.shape[1]
    rest = place[:, count : count + 1].astype(F32)
    low = jnp.where(at, rest, 0.0)
    return place[:, :count].astype(F32) + low, low


def assemble_kernel(sizes, panel_ref, fields_ref, prec_ref, coef_ref, vec_ref,
                    diag_rows, diag_full, own_out, next_out, lows_out, scales_out, rhs_out,
                    send_ref, slabs, arriving, design, weighted, part, part_high, from_mate, half, from_space,
                    own_buf, next_buf, diag_buf, vec_buf,
                    slab_send, slab_recv, prec_sems, mate_send, mate_recv, half_send, half_recv, all_send, all_recv):
    n_times, n_space, n_obs = sizes
    mine, count = prec_ref.shape
    rows_dev = panel_ref.shape[0]
    capacity = send_ref.shape[1]
    slots = n_times * capacity
    tm, sp, ob = lax.axis_index("tm"), lax.axis_index("space"), lax.axis_index("obs")
    cell = sp * n_obs + ob
    cells = n_space * n_obs
    at = on_diagonal(mine, count, cell)
    greeted = [{"tm": turn(tm, k, n_times)} for k in range(1, n_times)] + cell_peers(sp, ob, n_space, n_obs)
    barrier = pltpu.get_barrier_semaphore()
    for device in greeted:
        pl.semaphore_signal(barrier, inc=1, device_id=device, device_id_type=MESH)

    node, route = fields_ref[0:1, :], fields_ref[1:2, :]
    weight, residual = fields_ref[2:3, :], fields_ref[3:4, :]
    weighted_res = (weight * residual).astype(BF16).astype(F32)
    groups = max(8, n_times)
    marks = lax.broadcasted_iota(jnp.int32, (groups, rows_dev), 0).astype(F32) == route
    earlier = lax.broadcasted_iota(jnp.int32, (rows_dev, rows_dev), 0) < lax.broadcasted_iota(
        jnp.int32, (rows_dev, rows_dev), 1
    )
    before = mm(jnp.where(marks, 1.0, 0.0).astype(BF16), jnp.where(earlier, 1.0, 0.0).astype(BF16))
    slot = route * capacity + jnp.sum(jnp.where(marks, before, 0.0), axis=0, keepdims=True)
    here = lax.broadcasted_iota(jnp.int32, (slots, rows_dev), 0).astype(F32) == slot
    pick = jnp.where(here, 1.0, 0.0).astype(BF16)
    hits = lax.broadcasted_iota(jnp.int32, (count, rows_dev), 0).astype(F32) == node
    packed = (mm(pick, panel_ref[...]) + mm(pick, jnp.where(hits, 1.0, 0.0).astype(BF16), NT)).astype(BF16)
    slot_weight = jnp.sum(jnp.where(here, weight, 0.0), axis=1, keepdims=True)
    slot_res = jnp.sum(jnp.where(here, weighted_res, 0.0), axis=1, keepdims=True)
    lane = lax.broadcasted_iota(jnp.int32, (slots, WIDE), 1)
    beside = jnp.where(lane == 0, slot_weight, jnp.where(lane == 1, slot_res, 0.0)).astype(BF16)
    for t in range(n_times):
        send_ref[t, :, :count] = packed[t * capacity : (t + 1) * capacity, :]
        send_ref[t, :, count:] = beside[t * capacity : (t + 1) * capacity, :]
    pl.semaphore_wait(barrier, len(greeted))

    moves = []

    def slab(k):
        there = turn(tm, k, n_times)
        return send(send_ref.at[there], slabs.at[tm], slab_send.at[k], slab_recv.at[k], {"tm": there})

    early, late = list(range(1, n_times, 2)), list(range(2, n_times, 2))
    for parity, first in ((0, early), (1, late)):
        @pl.when(lax.rem(tm, 2) == parity)
        def _():
            for k in first:
                slab(k).start()

    coef = coef_ref[0:1, 0:1]
    coef_high = coef.astype(BF16).astype(F32)
    coef_mid = (coef - coef_high).astype(BF16).astype(F32)
    pack(prec_ref[...], own_buf.at[cell], at, (coef_high, coef_mid, coef - coef_high - coef_mid))
    prec_move = send(own_buf.at[cell], arriving, prec_sems.at[0], prec_sems.at[1], {"tm": turn(tm, -1, n_times)})
    even = lax.rem(tm, 2) == 0

    @pl.when(even)
    def _():
        prec_move.start()

    both = (all_send, all_recv)
    spreads = [Spread(buf, both, i, (n_space, n_obs)) for i, buf in enumerate((own_buf, next_buf, diag_buf, vec_buf))]
    own_spread, next_spread, diag_spread, vec_spread = spreads
    own_spread.start()
    slabs[tm] = send_ref[tm]
    for parity, first, second in ((0, early, late), (1, late, early)):
        @pl.when(lax.rem(tm, 2) == parity)
        def _():
            for k in first:
                slab(k).wait_send()
            if parity == 1:
                prec_move.start()
            for k in second:
                slab(k).start()

    prec_move.wait_recv()
    next_buf[cell] = arriving[...]
    next_spread.start()
    own_spread.forward()
    for k in range(1, n_times):
        place = slabs.at[turn(tm, -k, n_times)]
        send(place, place, slab_send.at[k], slab_recv.at[k], {"tm": tm}).wait_recv()

    grad = jnp.zeros((1, count), F32)
    for t in range(n_times):
        held = slabs[t]
        rows = held[:, :count].astype(F32)
        design[:, t * capacity : (t + 1) * capacity] = rows.T.astype(BF16)
        weighted[t * capacity : (t + 1) * capacity, :] = (held[:, count : count + 1].astype(F32) * rows).astype(BF16)
        grad = grad + jnp.sum(held[:, count + 1 : count + 2].astype(F32) * rows, axis=0, keepdims=True)
    vec_buf[cell] = vec_ref[...] + jnp.broadcast_to(grad, (8, count))
    vec_spread.start()
    for o in range(n_obs):
        for s in range(n_space):
            first = (s * n_obs + o) * mine
            value = mm(design[first : first + mine, :], weighted[...])
            part[o, s] = value
            part_high[o, s] = value.astype(BF16)
    for o in range(1, n_obs):
        mate = turn(ob, o, n_obs)
        move = send(part_high.at[mate], from_mate.at[o], mate_send.at[o], mate_recv.at[o], {"obs": mate})
        move.start()
        moves.append(move)
    next_spread.forward()
    vec_spread.forward()
    for o in range(1, n_obs):
        place = from_mate.at[o]
        send(place, place, mate_send.at[o], mate_recv.at[o], {"obs": ob}).wait_recv()

    def chip_sum(s):
        value = part[ob, s]
        for o in range(1, n_obs):
            value = value + from_mate[o, s].astype(F32)
        return value

    for k in range(1, n_space):
        there = turn(sp, k, n_space)
        half[k] = chip_sum(there).astype(BF16)
        move = send(half.at[k], from_space.at[k], half_send.at[k], half_recv.at[k], {"space": there})
        move.start()
        moves.append(move)
    gram = chip_sum(sp)
    next_rows, _ = unpack(next_buf.at[cell], at)
    three = next_buf[cell, :, count + 1 : count + 4].astype(F32)
    next_coef = jnp.sum(three, axis=1, keepdims=True)
    base = prec_ref[...] + next_coef * next_coef * next_rows + gram
    for k in range(1, n_space):
        place = from_space.at[k]
        send(place, place, half_send.at[k], half_recv.at[k], {"space": sp}).wait_recv()
        base = base + from_space[k].astype(F32)
    diag_rows[...] = base
    pack(base, diag_buf.at[cell], at, ())
    diag_spread.start()
    scales_out[0:1, :] = jnp.broadcast_to(-coef, (1, WIDE))
    scales_out[1:2, :] = jnp.broadcast_to(-next_coef[0:1, :], (1, WIDE))
    scales_out[2:8, :] = jnp.zeros((6, WIDE), F32)
    own_spread.finish()
    next_spread.finish()
    vec_spread.finish()
    total = vec_buf[0]
    for c in range(1, cells):
        total = total + vec_buf[c]
    rhs_out[...] = total
    def emit(at_row, buf, out):
        low_sum = jnp.zeros((1, count), F32)
        for c in range(cells):
            _, low = unpack(buf.at[c], on_diagonal(mine, count, c))
            low_sum = low_sum + jnp.sum(low, axis=0, keepdims=True)
            out[c * mine : (c + 1) * mine, :] = buf[c, :, :count]
        lows_out[at_row : at_row + 8, :] = jnp.broadcast_to(low_sum, (8, count))

    emit(0, own_buf, own_out)
    emit(8, next_buf, next_out)
    diag_spread.forward()
    diag_spread.finish()
    emit(16, diag_buf, diag_full)
    prec_move.wait_send()
    for parity, second in ((0, late), (1, early)):
        @pl.when(lax.rem(tm, 2) == parity)
        def _():
            for k in second:
                slab(k).wait_send()

    for move in moves:
        move.wait_send()


def assemble(sizes, panel, fields, prec, coef, vec):
    n_times, n_space, n_obs = sizes
    mine, count = prec.shape
    capacity = 2 * panel.shape[0] // n_times
    cells = n_space * n_obs
    slots = n_times * capacity
    vmem = pl.BlockSpec(memory_space=pltpu.VMEM)
    dma = pltpu.SemaphoreType.DMA
    wide = (cells, mine, count + WIDE)
    return pl.pallas_call(
        functools.partial(assemble_kernel, sizes),
        out_shape=(
            jax.ShapeDtypeStruct((mine, count), F32),
            jax.ShapeDtypeStruct((count, count), BF16),
            jax.ShapeDtypeStruct((count, count), BF16),
            jax.ShapeDtypeStruct((count, count), BF16),
            jax.ShapeDtypeStruct((24, count), F32),
            jax.ShapeDtypeStruct((8, WIDE), F32),
            jax.ShapeDtypeStruct((8, count), F32),
        ),
        in_specs=[vmem] * 5,
        out_specs=(vmem,) * 7,
        scratch_shapes=[
            pltpu.VMEM((n_times, capacity, count + WIDE), BF16),
            pltpu.VMEM((n_times, capacity, count + WIDE), BF16),
            pltpu.VMEM((mine, count + WIDE), BF16),
            pltpu.VMEM((count, slots), BF16),
            pltpu.VMEM((slots, count), BF16),
            pltpu.VMEM((n_obs, n_space, mine, count), F32),
            pltpu.VMEM((n_obs, n_space, mine, count), BF16),
            pltpu.VMEM((n_obs, n_space, mine, count), BF16),
            pltpu.VMEM((n_space, mine, count), BF16),
            pltpu.VMEM((n_space, mine, count), BF16),
            pltpu.VMEM(wide, BF16),
            pltpu.VMEM(wide, BF16),
            pltpu.VMEM(wide, BF16),
            pltpu.VMEM((cells, 8, count), F32),
            dma((n_times,)),
            dma((n_times,)),
            dma((2,)),
            dma((n_obs,)),
            dma((n_obs,)),
            dma((n_space,)),
            dma((n_space,)),
            dma((4, n_space, n_obs)),
            dma((4, n_space, n_obs)),
        ],
        compiler_params=pltpu.CompilerParams(
            collective_id=0, has_side_effects=True, vmem_limit_bytes=32 * 1024 * 1024
        ),
    )(panel, fields, prec, coef, vec)


def reduce_kernel(sizes, by_left, by_right, up_left, up_right, diag_ref, rhs_ref,
                  diag_rows, diag_full, left_out, right_out, lows_out, rhs_out,
                  to_left, to_right, loss_left, loss_right, in_up_left, in_up_right,
                  left_buf, right_buf, diag_buf, vec_buf,
                  send_sems, recv_sems, all_send, all_recv):
    n_times, n_space, n_obs = sizes
    mine, count = diag_ref.shape
    tm, sp, ob = lax.axis_index("tm"), lax.axis_index("space"), lax.axis_index("obs")
    cell = sp * n_obs + ob
    cells = n_space * n_obs
    left, right = {"tm": turn(tm, -1, n_times)}, {"tm": turn(tm, 1, n_times)}
    greet([left, right] + cell_peers(sp, ob, n_space, n_obs))
    kind = lax.rem(tm, 4)

    def fill_copy(is_left):
        buf, source = (right_buf, to_left) if is_left else (left_buf, to_right)
        which = 3 if is_left else 0
        return send(source.at[1], buf.at[cell], send_sems.at[which], recv_sems.at[which], left if is_left else right)

    def loss_copy(is_left):
        buf, source = (loss_right, to_left) if is_left else (loss_left, to_right)
        which = 4 if is_left else 1
        return send(source.at[0], buf, send_sems.at[which], recv_sems.at[which], left if is_left else right)

    def up_copy(is_left):
        buf, source = (in_up_right, up_left) if is_left else (in_up_left, up_right)
        which = 5 if is_left else 2
        return send(source, buf, send_sems.at[which], recv_sems.at[which], left if is_left else right)

    for middle_left in (False, True):
        @pl.when(kind == (3 if middle_left else 1))
        def _():
            near = to_left if middle_left else to_right
            if middle_left:
                near[1] = (-by_left[mine:, :]).astype(BF16)
            else:
                near[1] = (-by_right[:mine, :]).astype(BF16)
            first = fill_copy(middle_left)
            first.start()
            near[0] = (by_left[:mine, :] if middle_left else by_right[mine:, :]).astype(BF16)
            second = loss_copy(middle_left)
            second.start()
            third = up_copy(middle_left)
            third.start()
            far = to_right if middle_left else to_left
            far[0] = (by_right[mine:, :] if middle_left else by_left[:mine, :]).astype(BF16)
            first.wait_send()
            second.wait_send()
            others = [loss_copy(not middle_left), up_copy(not middle_left)]
            for move in others:
                move.start()
            for move in [third] + others:
                move.wait_send()

    @pl.when(kind != 2)
    def _():
        rhs_out[...] = rhs_ref[...]

    @pl.when(kind % 2 == 1)
    def _():
        diag_rows[...] = diag_ref[...]

    @pl.when(kind == 0)
    def _():
        for is_left in (False, True):
            loss_copy(is_left).wait_recv()
            up_copy(is_left).wait_recv()
        diag_rows[...] = diag_ref[...] - loss_left[...].astype(F32) - loss_right[...].astype(F32)
        rhs_out[...] = rhs_ref[...] - in_up_left[...] - in_up_right[...]

    @pl.when(kind == 2)
    def _():
        both = (all_send, all_recv)
        spreads = [
            Spread(buf, both, i, (n_space, n_obs)) for i, buf in enumerate((left_buf, right_buf, diag_buf, vec_buf))
        ]
        fill_copy(False).wait_recv()
        spreads[0].start()
        fill_copy(True).wait_recv()
        spreads[1].start()
        loss_copy(False).wait_recv()
        loss_copy(True).wait_recv()
        base = diag_ref[...] - loss_left[...].astype(F32) - loss_right[...].astype(F32)
        diag_rows[...] = base
        pack(base, diag_buf.at[cell], on_diagonal(mine, count, cell), ())
        spreads[2].start()
        up_copy(False).wait_recv()
        up_copy(True).wait_recv()
        vec_buf[cell] = in_up_left[...] + in_up_right[...]
        spreads[3].start()
        for spread in spreads:
            spread.forward()
        for spread in spreads:
            spread.finish()
        total = rhs_ref[...]
        low_sum = jnp.zeros((1, count), F32)
        for c in range(cells):
            total = total - vec_buf[c]
            left_out[c * mine : (c + 1) * mine, :] = left_buf[c]
            right_out[c * mine : (c + 1) * mine, :] = right_buf[c]
            _, low = unpack(diag_buf.at[c], on_diagonal(mine, count, c))
            low_sum = low_sum + jnp.sum(low, axis=0, keepdims=True)
            diag_full[c * mine : (c + 1) * mine, :] = diag_buf[c, :, :count]
        lows_out[:16, :] = jnp.zeros((16, count), F32)
        lows_out[16:, :] = jnp.broadcast_to(low_sum, (8, count))
        rhs_out[...] = total


def reduce_level(sizes, by_left, by_right, up_left, up_right, diag, rhs):
    n_times, n_space, n_obs = sizes
    mine, count = diag.shape
    cells = n_space * n_obs
    vmem = pl.BlockSpec(memory_space=pltpu.VMEM)
    dma = pltpu.SemaphoreType.DMA
    return pl.pallas_call(
        functools.partial(reduce_kernel, sizes),
        out_shape=(
            jax.ShapeDtypeStruct((mine, count), F32),
            jax.ShapeDtypeStruct((count, count), BF16),
            jax.ShapeDtypeStruct((count, count), BF16),
            jax.ShapeDtypeStruct((count, count), BF16),
            jax.ShapeDtypeStruct((24, count), F32),
            jax.ShapeDtypeStruct((8, count), F32),
        ),
        in_specs=[vmem] * 6,
        out_specs=(vmem,) * 6,
        scratch_shapes=[
            pltpu.VMEM((2, mine, count), BF16),
            pltpu.VMEM((2, mine, count), BF16),
            pltpu.VMEM((mine, count), BF16),
            pltpu.VMEM((mine, count), BF16),
            pltpu.VMEM((8, count), F32),
            pltpu.VMEM((8, count), F32),
            pltpu.VMEM((cells, mine, count), BF16),
            pltpu.VMEM((cells, mine, count), BF16),
            pltpu.VMEM((cells, mine, count + WIDE), BF16),
            pltpu.VMEM((cells, 8, count), F32),
            dma((6,)),
            dma((6,)),
            dma((4, n_space, n_obs)),
            dma((4, n_space, n_obs)),
        ],
        compiler_params=pltpu.CompilerParams(
            collective_id=1, has_side_effects=True, vmem_limit_bytes=20 * 1024 * 1024
        ),
    )(by_left, by_right, up_left, up_right, diag, rhs)


def last_kernel(n_times, by_left, by_right, up_left, up_right, loss_out, up_out,
                loss_send, loss_recv, up_send, up_recv, sems):
    mine = loss_out.shape[0]
    tm = lax.axis_index("tm")
    ways = [-2] if n_times == 4 else [-2, 2]
    greet([{"tm": turn(tm, way, n_times)} for way in ways])
    kind = lax.rem(tm, 4)

    def copies(i, way):
        device = {"tm": turn(tm, way, n_times)}
        return [
            send(loss_send.at[i], loss_recv.at[i], sems.at[0, i], sems.at[1, i], device),
            send(up_send.at[i], up_recv.at[i], sems.at[2, i], sems.at[3, i], device),
        ]

    @pl.when(kind == 2)
    def _():
        if n_times == 4:
            loss_send[0] = (by_left[:mine, :] + by_right[mine:, :]).astype(BF16)
            up_send[0] = up_left[...] + up_right[...]
        else:
            loss_send[0] = by_left[:mine, :].astype(BF16)
            loss_send[1] = by_right[mine:, :].astype(BF16)
            up_send[0] = up_left[...]
            up_send[1] = up_right[...]
        moves = [move for i, way in enumerate(ways) for move in copies(i, way)]
        for move in moves:
            move.start()
        for move in moves:
            move.wait_send()

    @pl.when(kind == 0)
    def _():
        for i, way in enumerate(ways):
            for move in copies(i, way):
                move.wait_recv()
        loss = loss_recv[0].astype(F32)
        up = up_recv[0]
        for i in range(1, len(ways)):
            loss = loss + loss_recv[i].astype(F32)
            up = up + up_recv[i]
        loss_out[...] = loss
        up_out[...] = up

    @pl.when(kind != 0)
    def _():
        loss_out[...] = jnp.zeros_like(loss_out)
        up_out[...] = jnp.zeros_like(up_out)


def last_level(n_times, by_left, by_right, up_left, up_right):
    many, count = by_left.shape
    mine = many // 2
    ways = 1 if n_times == 4 else 2
    vmem = pl.BlockSpec(memory_space=pltpu.VMEM)
    return pl.pallas_call(
        functools.partial(last_kernel, n_times),
        out_shape=(jax.ShapeDtypeStruct((mine, count), F32), jax.ShapeDtypeStruct((8, count), F32)),
        in_specs=[vmem] * 4,
        out_specs=(vmem, vmem),
        scratch_shapes=[
            pltpu.VMEM((ways, mine, count), BF16),
            pltpu.VMEM((ways, mine, count), BF16),
            pltpu.VMEM((ways, 8, count), F32),
            pltpu.VMEM((ways, 8, count), F32),
            pltpu.SemaphoreType.DMA((4, ways)),
        ],
        compiler_params=pltpu.CompilerParams(
            collective_id=2, has_side_effects=True, vmem_limit_bytes=12 * 1024 * 1024
        ),
    )(by_left, by_right, up_left, up_right)


def local(sizes, obs_panel, node_index, weight, residual, route_time, spatial_prec, ar_coef, prior_rhs):
    n_times, n_space, n_obs = sizes
    time = lax.axis_index("tm")
    cell = lax.axis_index("space") * n_obs + lax.axis_index("obs")
    _, mine, count = spatial_prec.shape

    def placed(row):
        full = lax.dynamic_update_slice(jnp.zeros((1, count), F32), row, (0, cell * mine))
        return jnp.broadcast_to(full, (8, count))

    def mine_of(full):
        return lax.dynamic_slice(full, (0, cell * mine), (1, mine))[0]

    odd = time % 2 == 1
    middle = time % 4 == 2
    fields = jnp.stack([value.astype(F32) for value in (node_index, route_time, weight, residual)])
    fields = jnp.concatenate([fields, jnp.zeros_like(fields)], axis=0)
    coef = jnp.broadcast_to(ar_coef[:, None], (8, WIDE))
    diag_one, diag_full, full_left, full_right, lows, scales, rhs_one = assemble(
        sizes, obs_panel, fields, spatial_prec[0], coef, placed(prior_rhs)
    )
    by_left, by_right, up = solve(sizes, odd, diag_full, full_left, full_right, lows, scales, rhs_one)
    fill_one = -by_right[:mine]
    diag_two, diag_full, full_left, full_right, lows, rhs_two = reduce_level(
        sizes, by_left, by_right, placed(up[:1, :mine]), placed(up[:1, mine:]), diag_one, rhs_one
    )
    by_left, by_right, up = solve(
        sizes, middle, diag_full, full_left, full_right, lows, jnp.ones_like(scales), rhs_two
    )
    fill_two = -by_right[:mine]
    loss, back = last_level(n_times, by_left, by_right, placed(up[:1, :mine]), placed(up[:1, mine:]))
    fill = jnp.where(odd, fill_one, jnp.where(middle, fill_two, 0.0))
    return (diag_two - loss)[None], fill[None], (mine_of(rhs_two) - mine_of(back))[None]


def solution(mesh):
    rows = ("grp", "tm", "space", "obs")
    blocks = P(("grp", "tm"), CELLS, None)
    vectors = P(("grp", "tm"), CELLS)
    sizes = tuple(mesh.shape[name] for name in ("tm", "space", "obs"))
    return jax.shard_map(
        functools.partial(local, sizes),
        mesh=mesh,
        in_specs=(P(rows, None), P(rows), P(rows), P(rows), P(rows), blocks, P(("grp", "tm")), vectors),
        out_specs=(blocks, blocks, vectors),
        check_vma=False,
    )
```

```python
import functools

import jax
import jax.numpy as jnp
from jax import lax
from jax.experimental import pallas as pl
from jax.experimental.pallas import tpu as pltpu
from jax.sharding import PartitionSpec as P

F32 = jnp.float32
BF16 = jnp.bfloat16
NN = (((1,), (0,)), ((), ()))
NT = (((1,), (1,)), ((), ()))
MESH = pl.DeviceIdType.MESH
WIDE = 128
CELLS = ("space", "obs")
GOAL = 2e-3
DOUBLINGS = 12
REFINES = 6


def split(value):
    high = value.astype(BF16)
    return high, (value - high.astype(F32)).astype(BF16)


def mm(left, right, dims=NN):
    return lax.dot_general(left, right, dims, preferred_element_type=F32)


def mm_exact(left, right):
    return lax.dot_general(left, right, NN, precision=lax.Precision.HIGHEST, preferred_element_type=F32)


def solve_kernel(tile, sizes, active_ref, diag_ref, left_ref, right_ref, lows_ref, scales_ref,
                 out_left, out_right, up_ref, x, e, sq, g, gh, res):
    count = diag_ref.shape[0]
    many = g.shape[0]
    mine = many // 2
    tiles = count // tile
    cell = lax.axis_index("space") * sizes[2] + lax.axis_index("obs")

    def strip(i):
        return pl.ds(pl.multiple_of(i * tile, tile), tile)

    def eye(i):
        row = lax.broadcasted_iota(jnp.int32, (tile, count), 0) + i * tile
        col = lax.broadcasted_iota(jnp.int32, (tile, count), 1)
        return row == col

    def set_rows():
        at = on_diagonal(mine, count, cell)
        here = pl.ds(pl.multiple_of(cell * mine, 16), mine)
        res[:mine, :] = left_ref[here, :].astype(F32) + jnp.where(at, lows_ref[0:1, :], 0.0)
        res[mine:, :] = right_ref[here, :].astype(F32) + jnp.where(at, lows_ref[8:9, :], 0.0)

    def exact_diag(place):
        def body(i, _):
            place[strip(i), :] = diag_ref[strip(i), :].astype(F32) + jnp.where(eye(i), lows_ref[16:17, :], 0.0)
            return 0

        lax.fori_loop(0, tiles, body, 0)

    def sweeps():
        exact_diag(x)
        lane = lax.broadcasted_iota(jnp.int32, (1, count), 1)

        def sweep(k, _):
            pivot_row = x[pl.ds(k, 1), :]
            inv = 1.0 / jnp.sum(jnp.where(lane == k, pivot_row, 0.0), axis=1, keepdims=True)
            row = pivot_row * inv

            def body(i, _):
                part = x[strip(i), :]
                here = lax.broadcasted_iota(jnp.int32, (tile, 1), 0) + i * tile == k
                col = jnp.sum(jnp.where(lane == k, part, 0.0), axis=1, keepdims=True)
                new = jnp.where(lane == k, col * inv, part - col * row)
                x[strip(i), :] = jnp.where(here, jnp.where(lane == k, -inv, row), new)
                return 0

            return lax.fori_loop(0, tiles, body, 0)

        lax.fori_loop(0, count, sweep, 0)
        x[...] = -x[...]

    @pl.when(active_ref[0] == 1)
    def _():
        set_rows()

        def square(i, most):
            part = mm(diag_ref[...], diag_ref[:, strip(i)])
            sq[:, strip(i)] = part
            return jnp.maximum(most, jnp.max(jnp.sum(jnp.abs(part), axis=0)))

        most = lax.fori_loop(0, tiles, square, jnp.float32(0.0))
        bound = jnp.sqrt(jnp.full((1, 128), most, F32)) * 1.03
        scale = (1.9 / bound)[:, :1]

        def first(i, total):
            diag = diag_ref[strip(i), :].astype(F32) * scale
            one = jnp.where(eye(i), 1.0, 0.0)
            err = one - 2.0 * diag + (scale * scale) * sq[strip(i), :]
            x[strip(i), :] = scale * (2.0 * one - diag)
            e[0, strip(i), :] = err.astype(BF16)
            return total + jnp.sum(err * err)

        total = lax.fori_loop(0, tiles, first, jnp.float32(0.0))

        def more(state):
            step, total = state
            return (total > 2.0) & (step < DOUBLINGS)

        def double(state):
            step, _ = state
            now = lax.rem(step, 2)

            def body(i, total):
                part = x[:, strip(i)]
                x[:, strip(i)] = part + mm(e[now], part.astype(BF16))
                err = mm(e[now], e[now, :, strip(i)])
                e[1 - now, :, strip(i)] = err.astype(BF16)
                return total + jnp.sum(err * err)

            return step + 1, lax.fori_loop(0, tiles, body, jnp.float32(0.0))

        step, _ = lax.while_loop(more, double, (jnp.int32(0), total))
        last = lax.rem(step, 2)

        def finish(i, _):
            part = x[:, strip(i)]
            e[1 - last, :, strip(i)] = (part + mm(e[last], part.astype(BF16))).astype(BF16)
            return 0

        lax.fori_loop(0, tiles, finish, 0)
        inverse = 1 - last
        begin = mm(res[...].astype(BF16), e[inverse]).astype(BF16)
        gh[...] = begin
        g[...] = begin.astype(F32)

        def again(state):
            step, size = state
            return jnp.logical_not(size <= GOAL * GOAL) & (step < REFINES)

        def refine(state):
            step, _ = state
            done = gh[...]
            rest = res[...] - mm(done, diag_ref[...]) - done.astype(F32) * lows_ref[16:17, :]
            res[...] = rest
            more = mm(rest.astype(BF16), e[inverse]).astype(BF16)
            gh[...] = more
            more = more.astype(F32)
            value = g[...] + more
            g[...] = value
            norm = jnp.sum(value * value, axis=1, keepdims=True) + 1e-30
            return step + 1, jnp.max(jnp.sum(more * more, axis=1, keepdims=True) / norm)

        _, size = lax.while_loop(again, refine, (jnp.int32(0), jnp.float32(1.0)))

        @pl.when(jnp.logical_not(size <= GOAL * GOAL))
        def _():
            sweeps()
            exact_diag(sq)
            g[...] = jnp.zeros_like(g)

            def improve(_, carry):
                set_rows()
                rest = res[...] - mm_exact(g[...], sq[...])
                g[...] += mm_exact(rest, x[...])
                return carry

            lax.fori_loop(0, 3, improve, 0)

        left_scale, right_scale = scales_ref[0:1, 0:1], scales_ref[1:2, 0:1]
        top = lax.broadcasted_iota(jnp.int32, (many, 1), 0) < mine
        value = g[...] * jnp.where(top, left_scale, right_scale)
        high, low = split(value)
        gh[...] = high
        for out, full, scale, at in ((out_left, left_ref, left_scale, 0), (out_right, right_ref, right_scale, 8)):
            out[...] = (mm(gh[...], full[...], NT) + value * lows_ref[at : at + 1, :]) * scale
        rhs_high, rhs_low = split(lows_ref[24:, :])
        up_ref[...] = mm(rhs_high, gh[...], NT) + mm(rhs_low, gh[...], NT) + mm(rhs_high, low, NT)


def solve(sizes, active, diag, full_left, full_right, lows, scales):
    count = diag.shape[0]
    many = 2 * (count // (sizes[1] * sizes[2]))
    vmem = pl.BlockSpec(memory_space=pltpu.VMEM)
    tile = 256 if count % 256 == 0 else count
    return pl.pallas_call(
        functools.partial(solve_kernel, tile, sizes),
        out_shape=(
            jax.ShapeDtypeStruct((many, count), F32),
            jax.ShapeDtypeStruct((many, count), F32),
            jax.ShapeDtypeStruct((8, many), F32),
        ),
        in_specs=[pl.BlockSpec(memory_space=pltpu.SMEM)] + [vmem] * 5,
        out_specs=(vmem, vmem, vmem),
        scratch_shapes=[
            pltpu.VMEM((count, count), F32),
            pltpu.VMEM((2, count, count), BF16),
            pltpu.VMEM((count, count), F32),
            pltpu.VMEM((many, count), F32),
            pltpu.VMEM((many, count), BF16),
            pltpu.VMEM((many, count), F32),
        ],
        compiler_params=pltpu.CompilerParams(vmem_limit_bytes=28 * 1024 * 1024),
    )(active.astype(jnp.int32).reshape(1), diag, full_left, full_right, lows, scales)


def turn(value, by, size):
    return lax.rem(value + (by + size), size)


def send(source, target, send_sem, recv_sem, device):
    return pltpu.make_async_remote_copy(
        src_ref=source, dst_ref=target, send_sem=send_sem, recv_sem=recv_sem, device_id=device, device_id_type=MESH
    )


def greet(devices):
    barrier = pltpu.get_barrier_semaphore()
    for device in devices:
        pl.semaphore_signal(barrier, inc=1, device_id=device, device_id_type=MESH)
    pl.semaphore_wait(barrier, len(devices))


def cell_peers(sp, ob, n_space, n_obs):
    return [
        {"space": turn(sp, k, n_space), "obs": turn(ob, o, n_obs)}
        for k in range(n_space)
        for o in range(n_obs)
        if k or o
    ]


class Spread:
    def __init__(self, buf, sems, which, sizes):
        self.buf, self.n_space, self.n_obs = buf, *sizes
        self.send_sems, self.recv_sems = (sem.at[which] for sem in sems)
        self.sp, self.ob = lax.axis_index("space"), lax.axis_index("obs")
        self.sent = []

    def block(self, k, o):
        return self.buf.at[turn(self.sp, -k, self.n_space) * self.n_obs + turn(self.ob, -o, self.n_obs)]

    def copy(self, k, o, forward):
        source = self.block(k, 0) if forward else self.block(0, 0)
        device = {"obs": turn(self.ob, o, self.n_obs)} if forward else {"space": turn(self.sp, k, self.n_space)}
        made = send(source, source, self.send_sems.at[k, o], self.recv_sems.at[k, o], device)
        made.start()
        self.sent.append(made)

    def arrived(self, k, o):
        place = self.block(k, o)
        send(place, place, self.send_sems.at[k, o], self.recv_sems.at[k, o], {"obs": self.ob}).wait_recv()

    def start(self):
        for k in range(1, self.n_space):
            self.copy(k, 0, False)
        for o in range(1, self.n_obs):
            self.copy(0, o, True)

    def forward(self):
        for k in range(1, self.n_space):
            self.arrived(k, 0)
            for o in range(1, self.n_obs):
                self.copy(k, o, True)

    def finish(self):
        for k in range(self.n_space):
            for o in range(1, self.n_obs):
                self.arrived(k, o)
        for made in self.sent:
            made.wait_send()


def on_diagonal(mine, count, cell):
    row = lax.broadcasted_iota(jnp.int32, (mine, count), 0) + cell * mine
    return row == lax.broadcasted_iota(jnp.int32, (mine, count), 1)


def pack(value, place, at, extra):
    mine, count = value.shape
    high = value.astype(BF16)
    rest = jnp.sum(jnp.where(at, value - high.astype(F32), 0.0), axis=1, keepdims=True)
    lane = lax.broadcasted_iota(jnp.int32, (mine, WIDE), 1)
    beside = jnp.where(lane == 0, rest, 0.0)
    for index, column in enumerate(extra):
        beside = jnp.where(lane == index + 1, column, beside)
    place[:, :count] = high
    place[:, count:] = beside.astype(BF16)


def unpack(place, at):
    count = at.shape[1]
    rest = place[:, count : count + 1].astype(F32)
    low = jnp.where(at, rest, 0.0)
    return place[:, :count].astype(F32) + low, low


def assemble_kernel(sizes, panel_ref, fields_ref, prec_ref, coef_ref, vec_ref,
                    diag_rows, diag_full, own_out, next_out, lows_out, scales_out,
                    send_ref, slabs, arriving, design, weighted, part, part_high, from_mate, half, from_space,
                    own_buf, next_buf, diag_buf, vec_buf,
                    slab_send, slab_recv, prec_sems, mate_send, mate_recv, half_send, half_recv, all_send, all_recv):
    n_times, n_space, n_obs = sizes
    mine, count = prec_ref.shape
    rows_dev = panel_ref.shape[0]
    capacity = send_ref.shape[1]
    slots = n_times * capacity
    tm, sp, ob = lax.axis_index("tm"), lax.axis_index("space"), lax.axis_index("obs")
    cell = sp * n_obs + ob
    cells = n_space * n_obs
    at = on_diagonal(mine, count, cell)
    greeted = [{"tm": turn(tm, k, n_times)} for k in range(1, n_times)] + cell_peers(sp, ob, n_space, n_obs)
    barrier = pltpu.get_barrier_semaphore()
    for device in greeted:
        pl.semaphore_signal(barrier, inc=1, device_id=device, device_id_type=MESH)

    node, route = fields_ref[0:1, :], fields_ref[1:2, :]
    weight, residual = fields_ref[2:3, :], fields_ref[3:4, :]
    weighted_res = (weight * residual).astype(BF16).astype(F32)
    groups = max(8, n_times)
    marks = lax.broadcasted_iota(jnp.int32, (groups, rows_dev), 0).astype(F32) == route
    earlier = lax.broadcasted_iota(jnp.int32, (rows_dev, rows_dev), 0) < lax.broadcasted_iota(
        jnp.int32, (rows_dev, rows_dev), 1
    )
    before = mm(jnp.where(marks, 1.0, 0.0).astype(BF16), jnp.where(earlier, 1.0, 0.0).astype(BF16))
    slot = route * capacity + jnp.sum(jnp.where(marks, before, 0.0), axis=0, keepdims=True)
    here = lax.broadcasted_iota(jnp.int32, (slots, rows_dev), 0).astype(F32) == slot
    pick = jnp.where(here, 1.0, 0.0).astype(BF16)
    hits = lax.broadcasted_iota(jnp.int32, (count, rows_dev), 0).astype(F32) == node
    packed = (mm(pick, panel_ref[...]) + mm(pick, jnp.where(hits, 1.0, 0.0).astype(BF16), NT)).astype(BF16)
    slot_weight = jnp.sum(jnp.where(here, weight, 0.0), axis=1, keepdims=True)
    slot_res = jnp.sum(jnp.where(here, weighted_res, 0.0), axis=1, keepdims=True)
    lane = lax.broadcasted_iota(jnp.int32, (slots, WIDE), 1)
    beside = jnp.where(lane == 0, slot_weight, jnp.where(lane == 1, slot_res, 0.0)).astype(BF16)
    for t in range(n_times):
        send_ref[t, :, :count] = packed[t * capacity : (t + 1) * capacity, :]
        send_ref[t, :, count:] = beside[t * capacity : (t + 1) * capacity, :]
    pl.semaphore_wait(barrier, len(greeted))

    moves = []

    def slab(k):
        there = turn(tm, k, n_times)
        return send(send_ref.at[there], slabs.at[tm], slab_send.at[k], slab_recv.at[k], {"tm": there})

    early, late = list(range(1, n_times, 2)), list(range(2, n_times, 2))
    for parity, first in ((0, early), (1, late)):
        @pl.when(lax.rem(tm, 2) == parity)
        def _():
            for k in first:
                slab(k).start()

    coef = coef_ref[0:1, 0:1]
    coef_high = coef.astype(BF16).astype(F32)
    coef_mid = (coef - coef_high).astype(BF16).astype(F32)
    pack(prec_ref[...], own_buf.at[cell], at, (coef_high, coef_mid, coef - coef_high - coef_mid))
    prec_move = send(own_buf.at[cell], arriving, prec_sems.at[0], prec_sems.at[1], {"tm": turn(tm, -1, n_times)})
    even = lax.rem(tm, 2) == 0

    @pl.when(even)
    def _():
        prec_move.start()

    both = (all_send, all_recv)
    spreads = [Spread(buf, both, i, (n_space, n_obs)) for i, buf in enumerate((own_buf, next_buf, diag_buf, vec_buf))]
    own_spread, next_spread, diag_spread, vec_spread = spreads
    own_spread.start()
    slabs[tm] = send_ref[tm]
    for parity, first, second in ((0, early, late), (1, late, early)):
        @pl.when(lax.rem(tm, 2) == parity)
        def _():
            for k in first:
                slab(k).wait_send()
            if parity == 1:
                prec_move.start()
            for k in second:
                slab(k).start()

    prec_move.wait_recv()
    next_buf[cell] = arriving[...]
    next_spread.start()
    own_spread.forward()
    for k in range(1, n_times):
        place = slabs.at[turn(tm, -k, n_times)]
        send(place, place, slab_send.at[k], slab_recv.at[k], {"tm": tm}).wait_recv()

    grad = jnp.zeros((1, count), F32)
    for t in range(n_times):
        held = slabs[t]
        rows = held[:, :count].astype(F32)
        design[:, t * capacity : (t + 1) * capacity] = rows.T.astype(BF16)
        weighted[t * capacity : (t + 1) * capacity, :] = (held[:, count : count + 1].astype(F32) * rows).astype(BF16)
        grad = grad + jnp.sum(held[:, count + 1 : count + 2].astype(F32) * rows, axis=0, keepdims=True)
    vec_buf[cell] = vec_ref[...] + jnp.broadcast_to(grad, (8, count))
    vec_spread.start()
    for o in range(n_obs):
        for s in range(n_space):
            first = (s * n_obs + o) * mine
            value = mm(design[first : first + mine, :], weighted[...])
            part[o, s] = value
            part_high[o, s] = value.astype(BF16)
    for o in range(1, n_obs):
        mate = turn(ob, o, n_obs)
        move = send(part_high.at[mate], from_mate.at[o], mate_send.at[o], mate_recv.at[o], {"obs": mate})
        move.start()
        moves.append(move)
    next_spread.forward()
    vec_spread.forward()
    for o in range(1, n_obs):
        place = from_mate.at[o]
        send(place, place, mate_send.at[o], mate_recv.at[o], {"obs": ob}).wait_recv()

    def chip_sum(s):
        value = part[ob, s]
        for o in range(1, n_obs):
            value = value + from_mate[o, s].astype(F32)
        return value

    for k in range(1, n_space):
        there = turn(sp, k, n_space)
        half[k] = chip_sum(there).astype(BF16)
        move = send(half.at[k], from_space.at[k], half_send.at[k], half_recv.at[k], {"space": there})
        move.start()
        moves.append(move)
    gram = chip_sum(sp)
    next_rows, _ = unpack(next_buf.at[cell], at)
    three = next_buf[cell, :, count + 1 : count + 4].astype(F32)
    next_coef = jnp.sum(three, axis=1, keepdims=True)
    base = prec_ref[...] + next_coef * next_coef * next_rows + gram
    for k in range(1, n_space):
        place = from_space.at[k]
        send(place, place, half_send.at[k], half_recv.at[k], {"space": sp}).wait_recv()
        base = base + from_space[k].astype(F32)
    diag_rows[...] = base
    pack(base, diag_buf.at[cell], at, ())
    diag_spread.start()
    scales_out[0:1, :] = jnp.broadcast_to(-coef, (1, WIDE))
    scales_out[1:2, :] = jnp.broadcast_to(-next_coef[0:1, :], (1, WIDE))
    scales_out[2:8, :] = jnp.zeros((6, WIDE), F32)
    own_spread.finish()
    next_spread.finish()
    vec_spread.finish()
    total = vec_buf[0]
    for c in range(1, cells):
        total = total + vec_buf[c]
    lows_out[24:, :] = total
    def emit(at_row, buf, out):
        low_sum = jnp.zeros((1, count), F32)
        for c in range(cells):
            _, low = unpack(buf.at[c], on_diagonal(mine, count, c))
            low_sum = low_sum + jnp.sum(low, axis=0, keepdims=True)
            out[c * mine : (c + 1) * mine, :] = buf[c, :, :count]
        lows_out[at_row : at_row + 8, :] = jnp.broadcast_to(low_sum, (8, count))

    emit(0, own_buf, own_out)
    emit(8, next_buf, next_out)
    diag_spread.forward()
    diag_spread.finish()
    emit(16, diag_buf, diag_full)
    prec_move.wait_send()
    for parity, second in ((0, late), (1, early)):
        @pl.when(lax.rem(tm, 2) == parity)
        def _():
            for k in second:
                slab(k).wait_send()

    for move in moves:
        move.wait_send()


def assemble(sizes, panel, fields, prec, coef, vec):
    n_times, n_space, n_obs = sizes
    mine, count = prec.shape
    capacity = 2 * panel.shape[0] // n_times
    cells = n_space * n_obs
    slots = n_times * capacity
    vmem = pl.BlockSpec(memory_space=pltpu.VMEM)
    dma = pltpu.SemaphoreType.DMA
    wide = (cells, mine, count + WIDE)
    return pl.pallas_call(
        functools.partial(assemble_kernel, sizes),
        out_shape=(
            jax.ShapeDtypeStruct((mine, count), F32),
            jax.ShapeDtypeStruct((count, count), BF16),
            jax.ShapeDtypeStruct((count, count), BF16),
            jax.ShapeDtypeStruct((count, count), BF16),
            jax.ShapeDtypeStruct((32, count), F32),
            jax.ShapeDtypeStruct((8, WIDE), F32),
        ),
        in_specs=[vmem] * 5,
        out_specs=(vmem,) * 6,
        scratch_shapes=[
            pltpu.VMEM((n_times, capacity, count + WIDE), BF16),
            pltpu.VMEM((n_times, capacity, count + WIDE), BF16),
            pltpu.VMEM((mine, count + WIDE), BF16),
            pltpu.VMEM((count, slots), BF16),
            pltpu.VMEM((slots, count), BF16),
            pltpu.VMEM((n_obs, n_space, mine, count), F32),
            pltpu.VMEM((n_obs, n_space, mine, count), BF16),
            pltpu.VMEM((n_obs, n_space, mine, count), BF16),
            pltpu.VMEM((n_space, mine, count), BF16),
            pltpu.VMEM((n_space, mine, count), BF16),
            pltpu.VMEM(wide, BF16),
            pltpu.VMEM(wide, BF16),
            pltpu.VMEM(wide, BF16),
            pltpu.VMEM((cells, 8, count), F32),
            dma((n_times,)),
            dma((n_times,)),
            dma((2,)),
            dma((n_obs,)),
            dma((n_obs,)),
            dma((n_space,)),
            dma((n_space,)),
            dma((4, n_space, n_obs)),
            dma((4, n_space, n_obs)),
        ],
        compiler_params=pltpu.CompilerParams(
            collective_id=0, has_side_effects=True, vmem_limit_bytes=32 * 1024 * 1024
        ),
    )(panel, fields, prec, coef, vec)


def reduce_kernel(sizes, by_left, by_right, up_left, up_right, diag_ref, rhs_ref,
                  diag_rows, diag_full, left_out, right_out, lows_out,
                  to_left, to_right, loss_left, loss_right, in_up_left, in_up_right,
                  left_buf, right_buf, diag_buf, vec_buf,
                  send_sems, recv_sems, all_send, all_recv):
    n_times, n_space, n_obs = sizes
    mine, count = diag_ref.shape
    tm, sp, ob = lax.axis_index("tm"), lax.axis_index("space"), lax.axis_index("obs")
    cell = sp * n_obs + ob
    cells = n_space * n_obs
    left, right = {"tm": turn(tm, -1, n_times)}, {"tm": turn(tm, 1, n_times)}
    greet([left, right] + cell_peers(sp, ob, n_space, n_obs))
    kind = lax.rem(tm, 4)

    def fill_copy(is_left):
        buf, source = (right_buf, to_left) if is_left else (left_buf, to_right)
        which = 3 if is_left else 0
        return send(source.at[1], buf.at[cell], send_sems.at[which], recv_sems.at[which], left if is_left else right)

    def loss_copy(is_left):
        buf, source = (loss_right, to_left) if is_left else (loss_left, to_right)
        which = 4 if is_left else 1
        return send(source.at[0], buf, send_sems.at[which], recv_sems.at[which], left if is_left else right)

    def up_copy(is_left):
        buf, source = (in_up_right, up_left) if is_left else (in_up_left, up_right)
        which = 5 if is_left else 2
        return send(source, buf, send_sems.at[which], recv_sems.at[which], left if is_left else right)

    for middle_left in (False, True):
        @pl.when(kind == (3 if middle_left else 1))
        def _():
            near = to_left if middle_left else to_right
            if middle_left:
                near[1] = (-by_left[mine:, :]).astype(BF16)
            else:
                near[1] = (-by_right[:mine, :]).astype(BF16)
            first = fill_copy(middle_left)
            first.start()
            near[0] = (by_left[:mine, :] if middle_left else by_right[mine:, :]).astype(BF16)
            second = loss_copy(middle_left)
            second.start()
            third = up_copy(middle_left)
            third.start()
            far = to_right if middle_left else to_left
            far[0] = (by_right[mine:, :] if middle_left else by_left[:mine, :]).astype(BF16)
            first.wait_send()
            second.wait_send()
            others = [loss_copy(not middle_left), up_copy(not middle_left)]
            for move in others:
                move.start()
            for move in [third] + others:
                move.wait_send()

    @pl.when(kind != 2)
    def _():
        lows_out[24:, :] = rhs_ref[24:, :]

    @pl.when(kind % 2 == 1)
    def _():
        diag_rows[...] = diag_ref[...]

    @pl.when(kind == 0)
    def _():
        for is_left in (False, True):
            loss_copy(is_left).wait_recv()
            up_copy(is_left).wait_recv()
        diag_rows[...] = diag_ref[...] - loss_left[...].astype(F32) - loss_right[...].astype(F32)
        lows_out[24:, :] = rhs_ref[24:, :] - in_up_left[...] - in_up_right[...]

    @pl.when(kind == 2)
    def _():
        both = (all_send, all_recv)
        spreads = [
            Spread(buf, both, i, (n_space, n_obs)) for i, buf in enumerate((left_buf, right_buf, diag_buf, vec_buf))
        ]
        fill_copy(False).wait_recv()
        spreads[0].start()
        fill_copy(True).wait_recv()
        spreads[1].start()
        loss_copy(False).wait_recv()
        loss_copy(True).wait_recv()
        base = diag_ref[...] - loss_left[...].astype(F32) - loss_right[...].astype(F32)
        diag_rows[...] = base
        pack(base, diag_buf.at[cell], on_diagonal(mine, count, cell), ())
        spreads[2].start()
        up_copy(False).wait_recv()
        up_copy(True).wait_recv()
        vec_buf[cell] = in_up_left[...] + in_up_right[...]
        spreads[3].start()
        for spread in spreads:
            spread.forward()
        for spread in spreads:
            spread.finish()
        total = rhs_ref[24:, :]
        low_sum = jnp.zeros((1, count), F32)
        for c in range(cells):
            total = total - vec_buf[c]
            left_out[c * mine : (c + 1) * mine, :] = left_buf[c]
            right_out[c * mine : (c + 1) * mine, :] = right_buf[c]
            _, low = unpack(diag_buf.at[c], on_diagonal(mine, count, c))
            low_sum = low_sum + jnp.sum(low, axis=0, keepdims=True)
            diag_full[c * mine : (c + 1) * mine, :] = diag_buf[c, :, :count]
        lows_out[:16, :] = jnp.zeros((16, count), F32)
        lows_out[16:24, :] = jnp.broadcast_to(low_sum, (8, count))
        lows_out[24:, :] = total


def reduce_level(sizes, by_left, by_right, up_left, up_right, diag, rhs):
    n_times, n_space, n_obs = sizes
    mine, count = diag.shape
    cells = n_space * n_obs
    vmem = pl.BlockSpec(memory_space=pltpu.VMEM)
    dma = pltpu.SemaphoreType.DMA
    return pl.pallas_call(
        functools.partial(reduce_kernel, sizes),
        out_shape=(
            jax.ShapeDtypeStruct((mine, count), F32),
            jax.ShapeDtypeStruct((count, count), BF16),
            jax.ShapeDtypeStruct((count, count), BF16),
            jax.ShapeDtypeStruct((count, count), BF16),
            jax.ShapeDtypeStruct((32, count), F32),
        ),
        in_specs=[vmem] * 6,
        out_specs=(vmem,) * 5,
        scratch_shapes=[
            pltpu.VMEM((2, mine, count), BF16),
            pltpu.VMEM((2, mine, count), BF16),
            pltpu.VMEM((mine, count), BF16),
            pltpu.VMEM((mine, count), BF16),
            pltpu.VMEM((8, count), F32),
            pltpu.VMEM((8, count), F32),
            pltpu.VMEM((cells, mine, count), BF16),
            pltpu.VMEM((cells, mine, count), BF16),
            pltpu.VMEM((cells, mine, count + WIDE), BF16),
            pltpu.VMEM((cells, 8, count), F32),
            dma((6,)),
            dma((6,)),
            dma((4, n_space, n_obs)),
            dma((4, n_space, n_obs)),
        ],
        compiler_params=pltpu.CompilerParams(
            collective_id=1, has_side_effects=True, vmem_limit_bytes=20 * 1024 * 1024
        ),
    )(by_left, by_right, up_left, up_right, diag, rhs)


def last_kernel(n_times, by_left, by_right, up_left, up_right, loss_out, up_out,
                loss_send, loss_recv, up_send, up_recv, sems):
    mine = loss_out.shape[0]
    tm = lax.axis_index("tm")
    ways = [-2] if n_times == 4 else [-2, 2]
    greet([{"tm": turn(tm, way, n_times)} for way in ways])
    kind = lax.rem(tm, 4)

    def copies(i, way):
        device = {"tm": turn(tm, way, n_times)}
        return [
            send(loss_send.at[i], loss_recv.at[i], sems.at[0, i], sems.at[1, i], device),
            send(up_send.at[i], up_recv.at[i], sems.at[2, i], sems.at[3, i], device),
        ]

    @pl.when(kind == 2)
    def _():
        if n_times == 4:
            loss_send[0] = (by_left[:mine, :] + by_right[mine:, :]).astype(BF16)
            up_send[0] = up_left[...] + up_right[...]
        else:
            loss_send[0] = by_left[:mine, :].astype(BF16)
            loss_send[1] = by_right[mine:, :].astype(BF16)
            up_send[0] = up_left[...]
            up_send[1] = up_right[...]
        moves = [move for i, way in enumerate(ways) for move in copies(i, way)]
        for move in moves:
            move.start()
        for move in moves:
            move.wait_send()

    @pl.when(kind == 0)
    def _():
        for i, way in enumerate(ways):
            for move in copies(i, way):
                move.wait_recv()
        loss = loss_recv[0].astype(F32)
        up = up_recv[0]
        for i in range(1, len(ways)):
            loss = loss + loss_recv[i].astype(F32)
            up = up + up_recv[i]
        loss_out[...] = loss
        up_out[...] = up

    @pl.when(kind != 0)
    def _():
        loss_out[...] = jnp.zeros_like(loss_out)
        up_out[...] = jnp.zeros_like(up_out)


def last_level(n_times, by_left, by_right, up_left, up_right):
    many, count = by_left.shape
    mine = many // 2
    ways = 1 if n_times == 4 else 2
    vmem = pl.BlockSpec(memory_space=pltpu.VMEM)
    return pl.pallas_call(
        functools.partial(last_kernel, n_times),
        out_shape=(jax.ShapeDtypeStruct((mine, count), F32), jax.ShapeDtypeStruct((8, count), F32)),
        in_specs=[vmem] * 4,
        out_specs=(vmem, vmem),
        scratch_shapes=[
            pltpu.VMEM((ways, mine, count), BF16),
            pltpu.VMEM((ways, mine, count), BF16),
            pltpu.VMEM((ways, 8, count), F32),
            pltpu.VMEM((ways, 8, count), F32),
            pltpu.SemaphoreType.DMA((4, ways)),
        ],
        compiler_params=pltpu.CompilerParams(
            collective_id=2, has_side_effects=True, vmem_limit_bytes=12 * 1024 * 1024
        ),
    )(by_left, by_right, up_left, up_right)


def local(sizes, obs_panel, node_index, weight, residual, route_time, spatial_prec, ar_coef, prior_rhs):
    n_times, n_space, n_obs = sizes
    time = lax.axis_index("tm")
    cell = lax.axis_index("space") * n_obs + lax.axis_index("obs")
    _, mine, count = spatial_prec.shape

    def placed(row):
        full = lax.dynamic_update_slice(jnp.zeros((1, count), F32), row, (0, cell * mine))
        return jnp.broadcast_to(full, (8, count))

    def mine_of(full):
        return lax.dynamic_slice(full, (0, cell * mine), (1, mine))[0]

    odd = time % 2 == 1
    middle = time % 4 == 2
    fields = jnp.stack([value.astype(F32) for value in (node_index, route_time, weight, residual)])
    fields = jnp.concatenate([fields, jnp.zeros_like(fields)], axis=0)
    coef = jnp.broadcast_to(ar_coef[:, None], (8, WIDE))
    diag_one, diag_full, full_left, full_right, lows, scales = assemble(
        sizes, obs_panel, fields, spatial_prec[0], coef, placed(prior_rhs)
    )
    by_left, by_right, up = solve(sizes, odd, diag_full, full_left, full_right, lows, scales)
    fill_one = -by_right[:mine]
    diag_two, diag_full, full_left, full_right, lows = reduce_level(
        sizes, by_left, by_right, placed(up[:1, :mine]), placed(up[:1, mine:]), diag_one, lows
    )
    by_left, by_right, up = solve(
        sizes, middle, diag_full, full_left, full_right, lows, jnp.ones_like(scales)
    )
    fill_two = -by_right[:mine]
    loss, back = last_level(n_times, by_left, by_right, placed(up[:1, :mine]), placed(up[:1, mine:]))
    fill = jnp.where(odd, fill_one, jnp.where(middle, fill_two, 0.0))
    return (diag_two - loss)[None], fill[None], (mine_of(lows[24:]) - mine_of(back))[None]


def solution(mesh):
    rows = ("grp", "tm", "space", "obs")
    blocks = P(("grp", "tm"), CELLS, None)
    vectors = P(("grp", "tm"), CELLS)
    sizes = tuple(mesh.shape[name] for name in ("tm", "space", "obs"))
    return jax.shard_map(
        functools.partial(local, sizes),
        mesh=mesh,
        in_specs=(P(rows, None), P(rows), P(rows), P(rows), P(rows), blocks, P(("grp", "tm")), vectors),
        out_specs=(blocks, blocks, vectors),
        check_vma=False,
    )
```
